512 devices in a mesh: node: 128 (over y, z, core), dp: 4 (over x).
Axes of the slice: x: 4, y: 4, z: 16, core: 2. Of those that a mesh axis runs over, the one named last changes fastest.
Arguments:
- node_feats: bfloat16 [4, 128, 512, 256], P('dp', 'node'), may hold values from -6 to 6
- cotangent: bfloat16 [4, 128, 512, 256], P('dp', 'node'), may hold values from -6 to 6
- mesh_of_block: int32 [4, 128], P('dp', 'node'), may hold values from 0 to 15, as said below
- block_rows: int32 [4, 128], P('dp', 'node'), may hold values from 1 to 512
- ln_gain: float32 [256], replicated, may hold values from 0.5 to 1.5
- w_in_x: bfloat16 [256, 256], replicated, may hold values from -0.375 to 0.375
- w_in_fx: bfloat16 [256, 256], replicated, may hold values from -0.375 to 0.375
- w_slice: float32 [32, 64], replicated, may hold values from -1 to 1
- temper: float32 [8], replicated, may hold values from 0.25 to 1
- w_qkv: float32 [32, 96], replicated, may hold values from -1 to 1
- w_out: bfloat16 [256, 256], replicated, may hold values from -0.375 to 0.375
Outputs:
- feats_grad: bfloat16 [4, 128, 512, 256], P('dp', 'node')
- gain_grad: float32 [256], replicated
- in_x_grad: float32 [256, 256], replicated
- in_fx_grad: float32 [256, 256], replicated
- slice_grad: float32 [32, 64], replicated
- temper_grad: float32 [8], replicated
- qkv_grad: float32 [32, 96], replicated
- out_grad: float32 [256, 256], replicated
The draws below stay inside these ranges and needn't reach their ends.
Inputs may be any that keep to these rules, and one draw needn't show every extreme that they name: `mesh_of_block`: every mesh number of a group names at least one of its blocks.
All inputs are finite; a program needn't handle non-finite values.
Results may differ from the reference program's by a relative error of at most 0.02.
Values may be sent and summed in bfloat16 or wider, within the bound.
No kernel may reach another device: no remote copies, remote signals or barrier semaphores. Data moves between devices by JAX's collectives and lax.ppermute only.
A program may use at most 64 MiB of HBM per device.

```python
import math
import jax
import jax.numpy as jnp
from jax import lax

C = 256
H = 8
DH = 32
M = 64
BLOCK = 512
MESH_G = 16
GROUPS = 4
BLOCKS = 128


def draw_mesh_of_block(key, part):
    key = jax.random.fold_in(key, 11)
    first, second, third = jax.random.split(key, 3)
    left = jax.random.randint(first, (GROUPS, BLOCKS), 0, MESH_G)
    right = jax.random.randint(second, (GROUPS, BLOCKS), 0, MESH_G)
    labels = jnp.minimum(left, right)
    orders = jax.vmap(lambda k: jax.random.permutation(k, BLOCKS))(jax.random.split(third, GROUPS))
    seats = orders[:, :MESH_G]
    group_index = jnp.arange(GROUPS)[:, None]
    labels = labels.at[group_index, seats].set(jnp.broadcast_to(jnp.arange(MESH_G)[None, :], (GROUPS, MESH_G)))
    return labels.astype(jnp.int32)


def draw_block_rows(key, part):
    key = jax.random.fold_in(key, 23)
    first, second = jax.random.split(key, 2)
    partial_rows = jax.random.randint(first, (GROUPS, BLOCKS), 1, BLOCK + 1)
    filled = jax.random.randint(second, (GROUPS, BLOCKS), 0, 4)
    counts = jnp.where(filled > 0, BLOCK, partial_rows)
    counts = counts.at[:, 0].set(BLOCK)
    return counts.astype(jnp.int32)


def steps_of(key, extent, pieces, smallest, largest):
    def one(position, shards_of):
        heights = jax.random.uniform(jax.random.fold_in(jax.random.fold_in(key, 6), position), (shards_of,), jnp.float32, smallest / len(pieces), largest / len(pieces))
        return jnp.repeat(jnp.exp(heights), extent[position] // shards_of).reshape((-1,) + (1,) * (len(extent) - position - 1))

    gain = one(*pieces[0])
    for cut in pieces[1:]:
        gain = gain * one(*cut)
    return gain


def normal_values(key, shape, scale, limit, cuts=(), held_as=jnp.bfloat16):
    values = scale * jax.random.normal(key, shape, jnp.float32)
    if cuts:
        values = values * steps_of(key, shape, cuts, -0.22, 0.18)
    return jnp.clip(values, -limit, limit).astype(held_as)


def setup_inputs(seed: int = 0) -> dict:
    seeds = jax.random.split(jax.random.key(seed), 12)
    node_feats = normal_values(seeds[0], (GROUPS, BLOCKS, BLOCK, C), 1.0, 6.0, ((0, 4), (1, 128)))
    cotangent = normal_values(seeds[1], (GROUPS, BLOCKS, BLOCK, C), 1.0, 6.0, ((0, 4), (1, 128)))
    mesh_of_block = draw_mesh_of_block(jax.random.fold_in(seeds[11], 71), 0)
    block_rows = draw_block_rows(jax.random.fold_in(seeds[11], 71), 0)
    ln_gain = jnp.clip(1.0 + 0.1 * jax.random.normal(seeds[4], (C,), jnp.float32), 0.5, 1.5)
    w_in_x = normal_values(seeds[5], (C, C), C ** -0.5, 0.375)
    w_in_fx = normal_values(seeds[6], (C, C), C ** -0.5, 0.375)
    w_slice = normal_values(seeds[7], (DH, M), DH ** -0.5, 1.0, (), jnp.float32)
    temper = jnp.clip(jnp.exp(jax.random.uniform(seeds[8], (H,), jnp.float32, math.log(0.25), math.log(1.0))), 0.25, 1.0)
    w_qkv = normal_values(seeds[9], (DH, 3 * DH), DH ** -0.5, 1.0, (), jnp.float32)
    w_out = normal_values(seeds[10], (C, C), C ** -0.5, 0.375)
    return dict(node_feats=node_feats, cotangent=cotangent, mesh_of_block=mesh_of_block, block_rows=block_rows, ln_gain=ln_gain, w_in_x=w_in_x, w_in_fx=w_in_fx, w_slice=w_slice, temper=temper, w_qkv=w_qkv, w_out=w_out)


EPS_NORM = 1e-05
EPS_MASS = 1e-05

def build_masks(ids, rows, meshes, length):
    valid = (jnp.arange(length, dtype=jnp.int32)[None, :] < rows[:, None]).astype(jnp.float32)
    onehot = (ids[:, None] == jnp.arange(meshes, dtype=jnp.int32)[None, :]).astype(jnp.float32)
    return (valid, onehot)

def layer_norm(xf, ln_gain):
    mean = lax.optimization_barrier(jnp.mean(xf, axis=-1, keepdims=True))
    centered = xf - mean
    var = lax.optimization_barrier(jnp.mean(centered * centered, axis=-1, keepdims=True))
    return (centered * lax.rsqrt(var + EPS_NORM) * ln_gain).astype(jnp.bfloat16)

def slice_softmax(logits, temper, valid):
    heads = temper.shape[0]
    shape = logits.shape
    scaled = logits.reshape(shape[:-1] + (heads, shape[-1] // heads)) / temper[:, None]
    expo = jnp.exp(scaled)
    weights = expo / lax.optimization_barrier(jnp.sum(expo, axis=-1, keepdims=True)) * valid[..., None, None]
    weights = weights.reshape(shape)
    return (weights, weights.astype(jnp.bfloat16))

def collect(sw, feat, weights, onehot, heads):
    blocks, rows, width = feat.shape
    slices = sw.shape[-1] // heads
    per_block = jnp.einsum('bnhm,bnhd->bhmd', sw.astype(jnp.float32).reshape(blocks, rows, heads, slices), feat.astype(jnp.float32).reshape(blocks, rows, heads, width // heads), precision=lax.Precision.HIGHEST)
    mass_block = lax.optimization_barrier(jnp.sum(weights.reshape(blocks, rows, heads, slices), axis=1))
    table = jnp.einsum('bk,bhmd->khmd', onehot, per_block, precision=lax.Precision.HIGHEST)
    mass = jnp.einsum('bk,bhm->khm', onehot, mass_block, precision=lax.Precision.HIGHEST)
    return (table.reshape(-1, slices, width // heads), mass.reshape(-1, slices))

def attend(table, mass, w_qkv):
    width = table.shape[-1]
    token = table / (mass[..., None] + EPS_MASS)
    qkv = jnp.einsum('pmd,de->pme', token, w_qkv, precision=lax.Precision.HIGHEST)
    query = qkv[..., :width]
    keys = qkv[..., width:2 * width]
    values = qkv[..., 2 * width:]
    scores = jnp.einsum('pmd,pnd->pmn', query, keys, precision=lax.Precision.HIGHEST) / math.sqrt(width)
    expo = jnp.exp(scores)
    probs = expo / lax.optimization_barrier(jnp.sum(expo, axis=-1, keepdims=True))
    mixed = jnp.einsum('pmn,pnd->pmd', probs, values, precision=lax.Precision.HIGHEST)
    return mixed.astype(jnp.bfloat16)

def deslice(sw, mixed_f, onehot, heads):
    blocks, rows, total = sw.shape
    slices = total // heads
    width = mixed_f.shape[-1]
    chosen = jnp.einsum('bk,khmd->bhmd', onehot, mixed_f.reshape(-1, heads, slices, width), precision=lax.Precision.HIGHEST)
    out = jnp.einsum('bnhm,bhmd->bnhd', sw.astype(jnp.float32).reshape(blocks, rows, heads, slices), chosen, precision=lax.Precision.HIGHEST)
    return out.reshape(blocks, rows, heads * width).astype(jnp.bfloat16)

def contract_rows(left, right):
    flat_left = left.reshape(-1, left.shape[-1])
    flat_right = right.reshape(-1, right.shape[-1])
    return lax.dot_general(flat_left, flat_right, (((0,), (0,)), ((), ())), preferred_element_type=jnp.float32)

def contract_last(left, right):
    return lax.dot_general(left, right, (((2,), (1,)), ((), ())), preferred_element_type=jnp.float32)

def front(xf, valid, onehot, ln_gain, w_in_x, w_in_fx, w_slice, temper):
    heads = temper.shape[0]
    normed, ln_pull = jax.vjp(layer_norm, xf, ln_gain)
    mid = jnp.dot(normed, w_in_x, preferred_element_type=jnp.float32).astype(jnp.bfloat16)
    feat = jnp.dot(normed, w_in_fx, preferred_element_type=jnp.float32).astype(jnp.bfloat16)
    blockdiag = jnp.kron(jnp.eye(heads, dtype=jnp.float32), w_slice).astype(jnp.bfloat16)
    logits = jnp.dot(mid, blockdiag, preferred_element_type=jnp.float32)
    (weights, sw), soft_pull = jax.vjp(lambda lg, tp: slice_softmax(lg, tp, valid), logits, temper)
    sw = lax.optimization_barrier(sw)
    (table, mass), collect_pull = jax.vjp(lambda s, f, w: collect(s, f, w, onehot, heads), sw, feat, weights)
    saved = (normed, ln_pull, mid, blockdiag, soft_pull, collect_pull, sw)
    return (table, mass, saved)

def back(saved, d_sw_a, d_table, d_mass, g, w_in_x, w_in_fx):
    normed, ln_pull, mid, blockdiag, soft_pull, collect_pull, sw = saved
    heads_total = blockdiag.shape[1]
    width = blockdiag.shape[0]
    d_sw_b, d_feat, d_weights = collect_pull((d_table, d_mass))
    d_sw = (d_sw_a.astype(jnp.float32) + d_sw_b.astype(jnp.float32)).astype(jnp.bfloat16)
    d_logits, temper_grad = soft_pull((d_weights, d_sw))
    d_logits = d_logits.astype(jnp.bfloat16)
    heads = temper_grad.shape[0]
    slices = heads_total // heads
    head_size = width // heads
    d_block = contract_rows(mid, d_logits).reshape(heads, head_size, heads, slices)
    picks = jnp.arange(heads, dtype=jnp.int32)
    slice_grad = lax.optimization_barrier(jnp.sum(d_block[picks, :, picks, :], axis=0))
    d_mid = contract_last(d_logits, blockdiag).astype(jnp.bfloat16)
    in_x_grad = contract_rows(normed, d_mid)
    in_fx_grad = contract_rows(normed, d_feat)
    d_normed = (contract_last(d_mid, w_in_x) + contract_last(d_feat, w_in_fx)).astype(jnp.bfloat16)
    d_ln, gain_grad = ln_pull(d_normed)
    feats_grad = (g + d_ln).astype(jnp.bfloat16)
    return (feats_grad, gain_grad, in_x_grad, in_fx_grad, slice_grad, temper_grad)

def reference(node_feats, cotangent, mesh_of_block, block_rows, ln_gain, w_in_x, w_in_fx, w_slice, temper, w_qkv, w_out):
    heads = temper.shape[0]

    def group_step(group):
        group_feats, group_cot, ids, rows = group
        valid, onehot = build_masks(ids, rows, MESH_G, BLOCK)
        xf = group_feats.astype(jnp.float32)
        table, mass, saved = front(xf, valid, onehot, ln_gain, w_in_x, w_in_fx, w_slice, temper)
        mixed, attend_pull = jax.vjp(attend, table, mass, w_qkv)
        mixed = lax.optimization_barrier(mixed)
        mixed_f = mixed.astype(jnp.float32)
        out, deslice_pull = jax.vjp(lambda s, mf: deslice(s, mf, onehot, heads), saved[6], mixed_f)
        g = group_cot.astype(jnp.float32) * valid[..., None]
        g_b = g.astype(jnp.bfloat16)
        out_grad = contract_rows(out, g_b)
        d_out = contract_last(g_b, w_out).astype(jnp.bfloat16)
        d_sw_a, d_mixed_f = deslice_pull(d_out)
        d_table, d_mass, qkv_grad = attend_pull(d_mixed_f.astype(jnp.bfloat16))
        feats_grad, gain_grad, in_x_grad, in_fx_grad, slice_grad, temper_grad = back(saved, d_sw_a, d_table, d_mass, g, w_in_x, w_in_fx)
        return (feats_grad, (gain_grad, in_x_grad, in_fx_grad, slice_grad, temper_grad, qkv_grad, out_grad))
    feats_grad, grads = lax.map(group_step, (node_feats, cotangent, mesh_of_block, block_rows))
    gain_grad, in_x_grad, in_fx_grad, slice_grad, temper_grad, qkv_grad, out_grad = [lax.optimization_barrier(jnp.sum(item, axis=0)) for item in grads]
    return (feats_grad, gain_grad, in_x_grad, in_fx_grad, slice_grad, temper_grad, qkv_grad, out_grad)
```

```python
import math

import jax
import jax.numpy as jnp
from jax import lax
from jax.experimental import pallas as pl
from jax.experimental.pallas import tpu as pltpu
from jax.sharding import Mesh
from jax.sharding import PartitionSpec as P

EPS_NORM = 1e-05
EPS_MASS = 1e-05
HEADS = 8
DH = 32
SLICES = 64
WIDTH = 256
ROWS = 512
OWNERS = 8
PEERS = 32
SHARE = 8
BF16_MAX = 3.3895313892515355e38
F32 = jnp.float32
BF16 = jnp.bfloat16
HIGHEST = lax.Precision.HIGHEST


def iota(shape, dim):
    return lax.broadcasted_iota(jnp.int32, shape, dim)


def dot(a, b, dims=((1,), (0,)), precision=None):
    return lax.dot_general(a, b, (dims, ((), ())), precision=precision, preferred_element_type=F32)


def four_blocks(w_slice):
    two = jnp.concatenate([w_slice, w_slice], axis=1)
    four = jnp.concatenate([two, two], axis=1)
    tall = jnp.concatenate([four] * 4, axis=0)
    same = (iota((128, 256), 0) >> 5) == (iota((128, 256), 1) >> 6)
    return jnp.where(same, tall, 0.0).astype(BF16)


def head_ones():
    return ((iota((256, 256), 0) >> 6) == (iota((256, 256), 1) >> 6)).astype(F32).astype(BF16)


def fold_matrix():
    return ((iota((128, 128), 0) & 31) == (iota((128, 128), 1) & 31)).astype(F32).astype(BF16)


def quarter_mask(rows):
    return ((iota((rows, 128), 0) & 63) >> 4) == (iota((rows, 128), 1) >> 5)


def pack_rows(tiled):
    rows = tiled.shape[0]
    kept = jnp.where(quarter_mask(rows), tiled, 0.0)
    return jnp.sum(kept.reshape(rows // 64, 4, 16, 128), axis=1)


def spread_rows(packed):
    heads = packed.shape[0]
    tall = jnp.broadcast_to(packed[:, None], (heads, 4, 16, 128)).reshape(heads * 64, 128)
    return jnp.where(quarter_mask(heads * 64), tall, 0.0)


def temper_row(temper, group):
    head = iota((1, 256), 1) >> 6
    row = jnp.zeros((1, 256), F32)
    for i in range(4):
        row = jnp.where(head == i, temper[:, 4 * group + i : 4 * group + i + 1], row)
    return row


def head_sums(values, ones):
    high = jnp.clip(values, -BF16_MAX, BF16_MAX).astype(BF16)
    low = (values - high.astype(F32)).astype(BF16)
    return dot(high, ones) + dot(low, ones)


def weights_of(mid, blocks, inv_temper, ones, valid):
    scaled = dot(mid, blocks) * inv_temper
    expo = jnp.exp(scaled)
    return scaled, expo / head_sums(expo, ones) * valid


def valid_column(rows_ref):
    return (iota((ROWS, 1), 0) < rows_ref[0]).astype(F32)


def normalise(x):
    xf = x.astype(F32)
    mean = jnp.mean(xf, axis=-1, keepdims=True)
    centered = xf - mean
    var = jnp.mean(centered * centered, axis=-1, keepdims=True)
    rstd = lax.rsqrt(var + EPS_NORM)
    return centered * rstd, rstd


def front_kernel(
    rows_ref, mesh_ref, x_hbm, gain_hbm, wx_hbm, wfx_hbm, slice_hbm, temper_hbm, cot_hbm, wout_hbm,
    send_ref, normed_ref, mid_ref, feat_ref, sw_ref, dout_ref, scaled_ref, weights_ref, xhat_ref, rstd_ref,
    gain_ref, wx_ref, wfx_ref, cot_ref, blocks_ref, temper_ref,
    x_ref, slice_ref, heat_ref, wout_ref, sems,
):
    sources = (x_hbm, gain_hbm, wx_hbm, wfx_hbm, slice_hbm, temper_hbm, cot_hbm, wout_hbm)
    targets = (x_ref, gain_ref, wx_ref, wfx_ref, slice_ref, heat_ref, cot_ref, wout_ref)
    copies = [pltpu.make_async_copy(a, b, sems.at[i]) for i, (a, b) in enumerate(zip(sources, targets))]
    for copy in copies:
        copy.start()
    valid = valid_column(rows_ref)
    ones = head_ones()
    copies[0].wait()
    xhat, rstd = normalise(x_ref[...])
    xhat_ref[...] = xhat
    rstd_ref[...] = rstd
    copies[1].wait()
    normed = (xhat * gain_ref[...]).astype(BF16)
    normed_ref[...] = normed
    copies[2].wait()
    mid = dot(normed, wx_ref[...]).astype(BF16)
    copies[3].wait()
    feat = dot(normed, wfx_ref[...]).astype(BF16)
    mid_ref[...] = mid
    feat_ref[...] = feat
    copies[4].wait()
    blocks = four_blocks(slice_ref[...])
    blocks_ref[...] = blocks
    copies[5].wait()
    heat = heat_ref[...]
    copies[6].wait()
    g_b = (cot_ref[...].astype(F32) * valid).astype(BF16)
    copies[7].wait()
    d_out = dot(g_b, wout_ref[...], ((1,), (1,))).astype(BF16)
    dout_ref[...] = d_out
    fold = fold_matrix()
    diagonal = (iota((256, 256), 0) >> 6) == ((iota((256, 256), 1) & 127) >> 5)
    tables, grads, masses = [], [], []
    for group in range(2):
        lanes = slice(group * 128, (group + 1) * 128)
        inv_temper = 1.0 / temper_row(heat, group)
        scaled, weights = weights_of(mid[:, lanes], blocks, inv_temper, ones, valid)
        sw = weights.astype(BF16)
        wide = slice(group * 256, (group + 1) * 256)
        temper_ref[:, wide] = inv_temper
        scaled_ref[:, wide] = scaled
        weights_ref[:, wide] = weights
        sw_ref[:, wide] = sw
        both = jnp.concatenate([feat[:, lanes], d_out[:, lanes]], axis=1)
        full = jnp.where(diagonal, dot(sw, both, ((0,), (0,))), 0.0).astype(BF16)
        tables.append(pack_rows(dot(full[:, :128], fold)))
        grads.append(pack_rows(dot(full[:, 128:], fold)))
        mass = jnp.sum(weights, axis=0, keepdims=True)
        for slab in range(2):
            pair = mass[:, slab * 128 : (slab + 1) * 128]
            masses += [pair, pltpu.roll(pair, 64, 1)]
    row = iota((8, 128), 0)
    mesh = mesh_ref[0]
    number = jnp.where(row == 1, ((mesh >> 1) + 1).astype(F32), 0.0)
    tails = [jnp.where(row == 0, mass, number)[None] for mass in masses]
    packed = [jnp.concatenate(tables, axis=0), jnp.concatenate(grads, axis=0), jnp.concatenate(tails, axis=0)]
    packed = jnp.concatenate(packed, axis=1)
    odd = (mesh & 1).astype(F32)
    both = jnp.concatenate([(packed * (1.0 - odd))[:, None], (packed * odd)[:, None]], axis=1)
    send_ref[...] = both.reshape(2 * HEADS, 40, 128).astype(BF16)


def dense_kernel(blocks_ref, out_ref):
    blocks = blocks_ref[...].astype(F32)
    numbers = blocks[:, 33:34, :]
    for k in range(OWNERS):
        out_ref[k] = jnp.sum(jnp.where(numbers == float(k + 1), blocks, 0.0), axis=0).astype(BF16)


def attend_kernel(sums_ref, qkv_ref, out_ref, grad_ref):
    sums = jnp.sum(sums_ref[...].astype(F32), axis=0)
    w_qkv = qkv_ref[...]
    eye = iota((SLICES, 128), 0) == iota((SLICES, 128), 1)
    mass = jnp.sum(jnp.where(eye, sums[32:33, :], 0.0), axis=1, keepdims=True)
    inv = 1.0 / (mass + EPS_MASS)

    def unfold(spread):
        return (spread[:, 0:32] + spread[:, 32:64]) + (spread[:, 64:96] + spread[:, 96:128])

    token = unfold(spread_rows(sums[None, 0:16, :])) * inv
    d_mixed = unfold(spread_rows(sums[None, 16:32, :])).astype(BF16).astype(F32)
    scale = 1.0 / math.sqrt(DH)
    query = dot(token, w_qkv[:, 0:32], precision=HIGHEST)
    keys = dot(token, w_qkv[:, 32:64], precision=HIGHEST)
    values = dot(token, w_qkv[:, 64:96], precision=HIGHEST)
    expo = jnp.exp(dot(query, keys, ((1,), (1,)), HIGHEST) * scale)
    probs = expo / jnp.sum(expo, axis=-1, keepdims=True)
    mixed = dot(probs, values, precision=HIGHEST)
    d_values = dot(probs, d_mixed, ((0,), (0,)), HIGHEST)
    d_probs = dot(d_mixed, values, ((1,), (1,)), HIGHEST)
    d_scores = probs * (d_probs - jnp.sum(probs * d_probs, axis=-1, keepdims=True)) * scale
    d_query = dot(d_scores, keys, precision=HIGHEST)
    d_keys = dot(d_scores, query, ((0,), (0,)), HIGHEST)
    d_qkv = jnp.concatenate([d_query, d_keys, d_values], axis=1)
    grad = dot(token, d_qkv, ((0,), (0,)), HIGHEST)
    grad_ref[...] = jnp.concatenate([grad, jnp.zeros((DH, 32), F32)], axis=1)
    d_token = dot(d_qkv, w_qkv, ((1,), (1,)), HIGHEST)
    d_table = d_token * inv
    d_mass = -jnp.sum(d_token * token, axis=1, keepdims=True) * inv

    def pack(values):
        return pack_rows(jnp.concatenate([values] * 4, axis=1))[0]

    tail = jnp.sum(jnp.where(eye, d_mass, 0.0), axis=0, keepdims=True)
    tail = jnp.where(iota((8, 128), 0) == 0, tail, 0.0)
    packed = jnp.concatenate([pack(mixed), pack(d_table), tail], axis=0).astype(BF16)
    out_ref[...] = jnp.broadcast_to(packed[None], (OWNERS, 40, 128))


def choose_kernel(blocks_ref, meshes_ref, out_ref):
    numbers = blocks_ref[...].astype(F32)[:, 33:34, :]
    meshes = meshes_ref[...].astype(F32)
    for b in range(2 * HEADS):
        chosen = jnp.zeros((40, 128), F32)
        for k in range(OWNERS):
            chosen = jnp.where(numbers[b] == float(k + 1), meshes[k], chosen)
        out_ref[b] = chosen.astype(BF16)


def back_kernel(
    rows_ref,
    normed_ref, mid_ref, feat_ref, sw_ref, dout_ref, scaled_ref, weights_ref, xhat_ref, rstd_ref,
    gain_ref, wx_ref, wfx_ref, cot_ref, blocks_ref, temper_ref, tokens_ref, qkv_grad_ref,
    feats_ref, mine_ref, other_ref,
):
    valid = valid_column(rows_ref)
    tokens = jnp.sum(tokens_ref[...].astype(F32).reshape(HEADS, 2, 40, 128), axis=1)
    blocks = blocks_ref[...]
    ones = head_ones()
    fold = fold_matrix()
    diagonal = (iota((256, 128), 0) >> 6) == (iota((256, 128), 1) >> 5)
    low_half = iota((1, 128), 1) < 64
    mid = mid_ref[...]
    feat = feat_ref[...]
    d_out = dout_ref[...]
    outs, d_mids, d_feats, slabs, temper_rows = [], [], [], [], []

    def block_of(packed):
        tiled = dot(spread_rows(packed).astype(BF16), fold)
        return jnp.where(diagonal, tiled, 0.0).astype(BF16)

    for group in range(2):
        lanes = slice(group * 128, (group + 1) * 128)
        heads = tokens[4 * group : 4 * group + 4]
        chosen = jnp.concatenate([block_of(heads[:, 0:16]), block_of(heads[:, 16:32])], axis=1)
        d_mass = [heads[i, 32:33, :] for i in range(4)]
        d_mass = jnp.concatenate(
            [jnp.where(low_half, d_mass[i], pltpu.roll(d_mass[i + 1], 64, 1)) for i in (0, 2)], axis=1
        )
        wide = slice(group * 256, (group + 1) * 256)
        sw = sw_ref[:, wide]
        pair = dot(sw, chosen)
        outs.append(pair[:, :128].astype(BF16))
        d_feats.append(pair[:, 128:].astype(BF16))
        left = jnp.concatenate([d_out[:, lanes], feat[:, lanes]], axis=1)
        d_sw = dot(left, chosen, ((1,), (1,))).astype(BF16).astype(F32)
        d_weights = d_sw + d_mass
        inv_temper = temper_ref[:, wide]
        scaled = scaled_ref[:, wide]
        weights = weights_ref[:, wide]
        d_scaled = weights * (d_weights - head_sums(weights * d_weights, ones))
        temper_rows.append(-jnp.sum(d_scaled * scaled, axis=0, keepdims=True) * inv_temper)
        d_logits = (d_scaled * inv_temper).astype(BF16)
        d_block = dot(mid[:, lanes], d_logits, ((0,), (0,)))
        for i in range(4):
            slabs.append(d_block[i * 32 : (i + 1) * 32, (i // 2) * 128 : (i // 2 + 1) * 128])
        d_mids.append(dot(d_logits, blocks, ((1,), (1,))).astype(BF16))
    slice_grad = jnp.where(
        low_half, (slabs[0] + slabs[2]) + (slabs[4] + slabs[6]), (slabs[1] + slabs[3]) + (slabs[5] + slabs[7])
    )
    d_mid = jnp.concatenate(d_mids, axis=1)
    d_feat = jnp.concatenate(d_feats, axis=1)
    g = cot_ref[...].astype(F32) * valid
    out_grad = dot(jnp.concatenate(outs, axis=1), g.astype(BF16), ((0,), (0,)))
    in_grads = dot(normed_ref[...], jnp.concatenate([d_mid, d_feat], axis=1), ((0,), (0,)))
    d_normed = dot(d_mid, wx_ref[...], ((1,), (1,))) + dot(d_feat, wfx_ref[...], ((1,), (1,)))
    d_normed = d_normed.astype(BF16).astype(F32)
    xhat = xhat_ref[...]
    gain_grad = jnp.sum(d_normed * xhat, axis=0, keepdims=True)
    d_xhat = d_normed * gain_ref[...]
    d_x = rstd_ref[...] * (
        d_xhat
        - jnp.mean(d_xhat, axis=-1, keepdims=True)
        - xhat * jnp.mean(d_xhat * xhat, axis=-1, keepdims=True)
    )
    feats_ref[...] = (g + d_x).astype(BF16)

    temper_grad = jnp.zeros((1, 128), F32)
    lane = iota((1, 128), 1)
    for group in range(2):
        head = iota((1, 256), 1) >> 6
        for i in range(4):
            total = jnp.sum(jnp.where(head == i, temper_rows[group], 0.0), axis=1, keepdims=True)
            temper_grad = jnp.where(lane == 4 * group + i, total, temper_grad)
    row = iota((8, 128), 0)
    vectors = jnp.where(row == 0, gain_grad[:, :128], jnp.where(row == 1, gain_grad[:, 128:], 0.0))
    vectors = jnp.where(row == 2, temper_grad, vectors)
    small = jnp.concatenate([slice_grad, qkv_grad_ref[...], vectors, jnp.zeros((184, 128), F32)], axis=0)
    halves = []
    for lanes, last in ((slice(0, 128), small), (slice(128, 256), jnp.zeros((WIDTH, 128), F32))):
        pieces = [out_grad[:, lanes], in_grads[:, :256][:, lanes], in_grads[:, 256:][:, lanes], last]
        halves.append(jnp.concatenate([piece.reshape(PEERS, SHARE, 128) for piece in pieces], axis=1))
    first = lax.axis_index("c") == 0
    mine_ref[...] = jnp.where(first, halves[0], halves[1]).astype(BF16)
    other_ref[...] = jnp.where(first, halves[1], halves[0]).astype(BF16)


def add_kernel(a_ref, b_ref, out_ref):
    out_ref[...] = (a_ref[...].astype(F32) + b_ref[...].astype(F32)).astype(BF16)


def sum_kernel(parts_ref, out_ref):
    total = jnp.sum(parts_ref[...].astype(F32), axis=0).astype(BF16)
    out_ref[...] = jnp.broadcast_to(total[None], out_ref.shape)


def finish_kernel(parts_ref, gain_ref, in_x_ref, in_fx_ref, slice_ref, temper_ref, qkv_ref, out_ref):
    parts = parts_ref[...].astype(F32)
    for at, ref in enumerate((out_ref, in_x_ref, in_fx_ref)):
        for half in range(2):
            piece = parts[half * PEERS : (half + 1) * PEERS, at * SHARE : (at + 1) * SHARE]
            ref[:, half * 128 : (half + 1) * 128] = piece.reshape(WIDTH, 128)
    small = parts[:PEERS, 3 * SHARE :].reshape(WIDTH, 128)
    slices = small[0:32]
    slice_ref[...] = slices[:, :64] + slices[:, 64:]
    qkv_ref[...] = small[32:64, :96]
    gain_ref[:, :128] = small[64:65]
    gain_ref[:, 128:] = small[65:66]
    temper_ref[...] = small[66:67, :8]


def call(kernel, name, inputs, outputs, scalars=0, far=False, scratch=()):
    specs = [pl.BlockSpec(memory_space=pltpu.SMEM)] * scalars
    specs += [pl.BlockSpec(memory_space=pltpu.HBM if far else pltpu.VMEM)] * (len(inputs) - scalars)
    single = not isinstance(outputs, (list, tuple))
    out_specs = pl.BlockSpec(memory_space=pltpu.VMEM)
    return pl.pallas_call(
        kernel,
        name=name,
        out_shape=outputs,
        in_specs=specs,
        out_specs=out_specs if single else [out_specs] * len(outputs),
        scratch_shapes=scratch,
        compiler_params=pltpu.CompilerParams(vmem_limit_bytes=48 * 1024 * 1024),
    )(*inputs)


def shape(dims, dtype=BF16):
    return jax.ShapeDtypeStruct(dims, dtype)


def shards(
    node_feats, cotangent, mesh_of_block, block_rows, ln_gain, w_in_x, w_in_fx, w_slice, temper, w_qkv, w_out
):
    x = node_feats.reshape(ROWS, WIDTH)
    cot = cotangent.reshape(ROWS, WIDTH)
    rows = block_rows.reshape(1)
    number = mesh_of_block.reshape(1)
    gain = ln_gain.reshape(1, WIDTH)
    wide = shape((ROWS, WIDTH))
    packets = shape((2 * HEADS, 40, 128))
    owned = shape((OWNERS, 40, 128))
    tall = shape((ROWS, 2 * WIDTH), F32)
    inputs = (x, gain, w_in_x, w_in_fx, w_slice, temper.reshape(1, HEADS), cot, w_out)
    far = [pltpu.with_memory_space_constraint(a, pltpu.HBM) for a in inputs]
    send, *kept = call(
        front_kernel,
        "front",
        (rows, number, *far),
        [
            packets, wide, wide, wide, shape((ROWS, 2 * WIDTH)), wide,
            tall, tall, shape((ROWS, WIDTH), F32), shape((ROWS, 1), F32),
            shape((1, WIDTH), F32), shape((WIDTH, WIDTH)), shape((WIDTH, WIDTH)), wide,
            shape((128, 256)), shape((1, 2 * WIDTH), F32),
        ],
        scalars=2,
        far=True,
        scratch=[pltpu.VMEM(inputs[i].shape, inputs[i].dtype) for i in (0, 4, 5, 7)]
        + [pltpu.SemaphoreType.DMA((len(far),))],
    )
    blocks = lax.all_to_all(send, ("y", "c", "zl"), 0, 0)
    dense = call(dense_kernel, "dense", (blocks,), owned)
    sums = lax.all_to_all(dense, "zh", 0, 0)
    answer, qkv_grad = call(attend_kernel, "attend", (sums, w_qkv), [owned, shape((DH, 128), F32)])
    meshes = lax.all_to_all(answer, "zh", 0, 0)
    chosen = call(choose_kernel, "choose", (blocks, meshes), packets)
    tokens = lax.all_to_all(chosen, ("y", "c", "zl"), 0, 0)
    share = shape((PEERS, 4 * SHARE, 128))
    feats_grad, mine, other = call(
        back_kernel, "back", (rows, *kept, tokens, qkv_grad), [wide, share, share], scalars=1
    )
    across = ("y", "zl", "x")
    other = lax.ppermute(other, "c", [(0, 1), (1, 0)])
    parts = call(add_kernel, "add_pair", (mine, other), share)
    parts = lax.all_to_all(parts, across, 0, 0)
    parts = call(sum_kernel, "sum_peers", (parts,), shape((OWNERS, 4 * SHARE, 128)))
    parts = lax.all_to_all(parts, "zh", 0, 0)
    parts = call(sum_kernel, "sum_z", (parts,), share)
    parts = lax.all_to_all(parts, across, 0, 0)
    parts = lax.all_gather(parts, "c", axis=0, tiled=True)
    square = shape((WIDTH, WIDTH), F32)
    gain_grad, in_x_grad, in_fx_grad, slice_grad, temper_grad, qkv_grad, out_grad = call(
        finish_kernel,
        "finish",
        (parts,),
        [
            shape((1, WIDTH), F32), square, square, shape((DH, SLICES), F32),
            shape((1, HEADS), F32), shape((DH, 3 * DH), F32), square,
        ],
    )
    return (
        feats_grad.reshape(1, 1, ROWS, WIDTH),
        gain_grad.reshape(WIDTH),
        in_x_grad,
        in_fx_grad,
        slice_grad,
        temper_grad.reshape(HEADS),
        qkv_grad,
        out_grad,
    )


def solution(mesh):
    groups = mesh.shape["dp"]
    devices = mesh.devices.reshape(4, OWNERS, 2, 2, groups)
    grid = Mesh(devices, ("y", "zh", "zl", "c", "x"))
    node = ("y", "zh", "zl", "c")
    blocks = P("x", node, None, None)
    scalars = P("x", node)
    return jax.shard_map(
        shards,
        mesh=grid,
        in_specs=(blocks, blocks, scalars, scalars) + (P(),) * 7,
        out_specs=(blocks,) + (P(),) * 7,
        check_vma=False,
    )
```

```python
import math

import jax
import jax.numpy as jnp
from jax import lax
from jax.experimental import pallas as pl
from jax.experimental.pallas import tpu as pltpu
from jax.sharding import Mesh
from jax.sharding import PartitionSpec as P

EPS_NORM = 1e-05
EPS_MASS = 1e-05
HEADS = 8
DH = 32
SLICES = 64
WIDTH = 256
ROWS = 512
OWNERS = 8
PEERS = 32
SHARE = 8
F32 = jnp.float32
BF16 = jnp.bfloat16
HIGHEST = lax.Precision.HIGHEST


def iota(shape, dim):
    return lax.broadcasted_iota(jnp.int32, shape, dim)


def dot(a, b, dims=((1,), (0,)), precision=None):
    return lax.dot_general(a, b, (dims, ((), ())), precision=precision, preferred_element_type=F32)


def four_blocks(w_slice):
    two = jnp.concatenate([w_slice, w_slice], axis=1)
    four = jnp.concatenate([two, two], axis=1)
    tall = jnp.concatenate([four] * 4, axis=0)
    same = (iota((128, 256), 0) >> 5) == (iota((128, 256), 1) >> 6)
    return jnp.where(same, tall, 0.0).astype(BF16)


def fold_matrix():
    return ((iota((128, 128), 0) & 31) == (iota((128, 128), 1) & 31)).astype(F32).astype(BF16)


def quarter_mask(rows):
    return ((iota((rows, 128), 0) & 63) >> 4) == (iota((rows, 128), 1) >> 5)


def pack_rows(tiled):
    rows = tiled.shape[0]
    kept = jnp.where(quarter_mask(rows), tiled, 0.0)
    return jnp.sum(kept.reshape(rows // 64, 4, 16, 128), axis=1)


def spread_rows(packed):
    heads = packed.shape[0]
    tall = jnp.broadcast_to(packed[:, None], (heads, 4, 16, 128)).reshape(heads * 64, 128)
    return jnp.where(quarter_mask(heads * 64), tall, 0.0)


def temper_column(temper, group):
    head = iota((256, 1), 0) >> 6
    column = jnp.zeros((256, 1), F32)
    for i in range(4):
        column = jnp.where(head == i, temper[:, 4 * group + i : 4 * group + i + 1], column)
    return column


def head_sums(values):
    rows, nodes = values.shape
    sums = jnp.sum(values.reshape(rows // 64, 64, nodes), axis=1, keepdims=True)
    return jnp.broadcast_to(sums, (rows // 64, 64, nodes)).reshape(rows, nodes)


def eye_mask():
    return iota((SLICES, 128), 0) == iota((SLICES, 128), 1)


def column_to_row(column):
    return jnp.sum(jnp.where(eye_mask(), column, 0.0), axis=0, keepdims=True)


def row_to_column(row):
    return jnp.sum(jnp.where(eye_mask(), row, 0.0), axis=1, keepdims=True)


def normalise(x):
    xf = x.astype(F32)
    mean = jnp.mean(xf, axis=-1, keepdims=True)
    centered = xf - mean
    var = jnp.mean(centered * centered, axis=-1, keepdims=True)
    rstd = lax.rsqrt(var + EPS_NORM)
    return centered * rstd, rstd


def front_kernel(
    rows_ref, mesh_ref, x_hbm, gain_hbm, wx_hbm, wfx_hbm, slice_hbm, temper_hbm, cot_hbm, wout_hbm,
    send_ref, normed_ref, mid_ref, feat_ref, sw_ref, dout_ref, scaled_ref, weights_ref, xhat_ref, rstd_ref,
    gain_ref, wx_ref, wfx_ref, g_ref, blocks_ref, temper_ref,
    x_ref, slice_ref, heat_ref, cot_ref, wout_ref, sems,
):
    sources = (x_hbm, gain_hbm, wx_hbm, wfx_hbm, slice_hbm, temper_hbm, cot_hbm, wout_hbm)
    targets = (x_ref, gain_ref, wx_ref, wfx_ref, slice_ref, heat_ref, cot_ref, wout_ref)
    copies = [pltpu.make_async_copy(a, b, sems.at[i]) for i, (a, b) in enumerate(zip(sources, targets))]
    for copy in copies:
        copy.start()
    copies[0].wait()
    xhat, rstd = normalise(x_ref[...])
    xhat_ref[...] = xhat
    rstd_ref[...] = rstd
    copies[1].wait()
    normed = (xhat * gain_ref[...]).astype(BF16)
    normed_ref[...] = normed
    copies[2].wait()
    mid = dot(wx_ref[...], normed, ((0,), (1,))).astype(BF16)
    copies[3].wait()
    feat = dot(normed, wfx_ref[...]).astype(BF16)
    mid_ref[...] = mid
    feat_ref[...] = feat
    copies[4].wait()
    blocks = four_blocks(slice_ref[...])
    blocks_ref[...] = blocks
    copies[5].wait()
    heat = heat_ref[...]
    copies[6].wait()
    g_b = jnp.where(iota((ROWS, 1), 0) < rows_ref[0, 0], cot_ref[...].astype(F32), 0.0).astype(BF16)
    g_ref[...] = g_b
    copies[7].wait()
    d_out = dot(g_b, wout_ref[...], ((1,), (1,))).astype(BF16)
    dout_ref[...] = d_out
    fold = fold_matrix()
    diagonal = (iota((256, 256), 0) >> 6) == ((iota((256, 256), 1) & 127) >> 5)
    valid = (iota((1, ROWS), 1) < rows_ref[0, 0]).astype(F32)
    tables, grads, masses = [], [], []
    for group in range(2):
        lanes = slice(group * 128, (group + 1) * 128)
        wide = slice(group * 256, (group + 1) * 256)
        inv_temper = 1.0 / temper_column(heat, group)
        temper_ref[wide, :] = inv_temper
        scaled = dot(blocks, mid[lanes], ((0,), (0,))) * inv_temper
        expo = jnp.exp(scaled)
        weights = expo / head_sums(expo) * valid
        sw = weights.astype(BF16)
        scaled_ref[wide, :] = scaled
        weights_ref[wide, :] = weights
        sw_ref[wide, :] = sw
        both = jnp.concatenate([feat[:, lanes], d_out[:, lanes]], axis=1)
        full = jnp.where(diagonal, dot(sw, both), 0.0).astype(BF16)
        tables.append(pack_rows(dot(full[:, :128], fold)))
        grads.append(pack_rows(dot(full[:, 128:], fold)))
        mass = jnp.sum(weights, axis=1, keepdims=True)
        masses += [column_to_row(mass[64 * i : 64 * i + 64]) for i in range(4)]
    row = iota((8, 128), 0)
    mesh = mesh_ref[0, 0]
    number = jnp.where(row == 1, ((mesh >> 1) + 1).astype(F32), 0.0)
    tails = [jnp.where(row == 0, mass, number)[None] for mass in masses]
    packed = [jnp.concatenate(tables, axis=0), jnp.concatenate(grads, axis=0), jnp.concatenate(tails, axis=0)]
    packed = jnp.concatenate(packed, axis=1)
    odd = (mesh & 1).astype(F32)
    both = jnp.concatenate([(packed * (1.0 - odd))[:, None], (packed * odd)[:, None]], axis=1)
    send_ref[...] = both.reshape(2 * HEADS, 40, 128).astype(BF16)


def dense_kernel(blocks_ref, out_ref):
    blocks = blocks_ref[...].astype(F32)
    numbers = blocks[:, 33:34, :]
    for k in range(OWNERS):
        out_ref[k] = jnp.sum(jnp.where(numbers == float(k + 1), blocks, 0.0), axis=0).astype(BF16)


def attend_kernel(sums_ref, qkv_ref, out_ref, token_ref, d_qkv_ref):
    sums = jnp.sum(sums_ref[...].astype(F32), axis=0)
    w_qkv = qkv_ref[...]
    mass = row_to_column(sums[32:33, :])
    inv = 1.0 / (mass + EPS_MASS)

    def unfold(spread):
        return (spread[:, 0:32] + spread[:, 32:64]) + (spread[:, 64:96] + spread[:, 96:128])

    token = unfold(spread_rows(sums[None, 0:16, :])) * inv
    d_mixed = unfold(spread_rows(sums[None, 16:32, :])).astype(BF16).astype(F32)
    scale = 1.0 / math.sqrt(DH)
    query = dot(token, w_qkv[:, 0:32], precision=HIGHEST)
    keys = dot(token, w_qkv[:, 32:64], precision=HIGHEST)
    values = dot(token, w_qkv[:, 64:96], precision=HIGHEST)
    expo = jnp.exp(dot(query, keys, ((1,), (1,)), HIGHEST) * scale)
    probs = expo / jnp.sum(expo, axis=-1, keepdims=True)
    mixed = dot(probs, values, precision=HIGHEST)
    d_values = dot(probs, d_mixed, ((0,), (0,)), HIGHEST)
    d_probs = dot(d_mixed, values, ((1,), (1,)), HIGHEST)
    d_scores = probs * (d_probs - jnp.sum(probs * d_probs, axis=-1, keepdims=True)) * scale
    d_query = dot(d_scores, keys, precision=HIGHEST)
    d_keys = dot(d_scores, query, ((0,), (0,)), HIGHEST)
    d_qkv = jnp.concatenate([d_query, d_keys, d_values], axis=1)
    token_ref[...] = token
    d_qkv_ref[...] = d_qkv
    d_token = dot(d_qkv, w_qkv, ((1,), (1,)), HIGHEST)
    d_table = d_token * inv
    d_mass = -jnp.sum(d_token * token, axis=1, keepdims=True) * inv

    def pack(values):
        return pack_rows(jnp.concatenate([values] * 4, axis=1))[0]

    tail = jnp.where(iota((8, 128), 0) == 0, column_to_row(d_mass), 0.0)
    packed = jnp.concatenate([pack(mixed), pack(d_table), tail], axis=0).astype(BF16)
    out_ref[...] = jnp.broadcast_to(packed[None], (OWNERS, 40, 128))


def choose_kernel(blocks_ref, meshes_ref, out_ref):
    numbers = blocks_ref[...].astype(F32)[:, 33:34, :]
    meshes = meshes_ref[...].astype(F32)
    for b in range(2 * HEADS):
        chosen = jnp.zeros((40, 128), F32)
        for k in range(OWNERS):
            chosen = jnp.where(numbers[b] == float(k + 1), meshes[k], chosen)
        out_ref[b] = chosen.astype(BF16)


def back_kernel(
    normed_ref, mid_ref, feat_ref, sw_ref, dout_ref, scaled_ref, weights_ref, g_ref, blocks_ref, temper_ref, tokens_ref,
    mine_ref, other_ref, dmid_ref, dfeat_ref, slice_ref, heat_ref,
):
    tokens = jnp.sum(tokens_ref[...].astype(F32).reshape(HEADS, 2, 40, 128), axis=1)
    blocks = blocks_ref[...]
    fold = fold_matrix()
    diagonal = (iota((256, 128), 0) >> 6) == (iota((256, 128), 1) >> 5)
    low_half = iota((1, 128), 1) < 64
    feat = feat_ref[...]
    d_out = dout_ref[...]
    outs, d_mids, d_feats, slabs = [], [], [], []
    temper_grad = jnp.zeros((1, 128), F32)
    lane = iota((1, 128), 1)

    def block_of(packed):
        tiled = dot(spread_rows(packed).astype(BF16), fold)
        return jnp.where(diagonal, tiled, 0.0).astype(BF16)

    for group in range(2):
        lanes = slice(group * 128, (group + 1) * 128)
        wide = slice(group * 256, (group + 1) * 256)
        heads = tokens[4 * group : 4 * group + 4]
        chosen = jnp.concatenate([block_of(heads[:, 0:16]), block_of(heads[:, 16:32])], axis=1)
        d_mass = jnp.concatenate([row_to_column(heads[i, 32:33, :]) for i in range(4)], axis=0)
        pair = dot(chosen, sw_ref[wide, :], ((0,), (0,)))
        outs.append(pair[:128].astype(BF16))
        d_feats.append(pair[128:].astype(BF16))
        left = jnp.concatenate([d_out[:, lanes], feat[:, lanes]], axis=1)
        d_sw = dot(chosen, left, ((1,), (1,))).astype(BF16).astype(F32)
        d_weights = d_sw + d_mass
        inv_temper = temper_ref[wide, :]
        weights = weights_ref[wide, :]
        d_scaled = weights * (d_weights - head_sums(weights * d_weights))
        products = jnp.sum((d_scaled * scaled_ref[wide, :]).reshape(4, SLICES, ROWS), axis=1)
        totals = jnp.sum(products, axis=1, keepdims=True)
        for i in range(4):
            total = -totals[i : i + 1] * inv_temper[64 * i : 64 * i + 1]
            temper_grad = jnp.where(lane == 4 * group + i, total, temper_grad)
        d_logits = (d_scaled * inv_temper).astype(BF16)
        d_block = dot(mid_ref[lanes, :], d_logits, ((1,), (1,)))
        for i in range(4):
            slabs.append(d_block[i * 32 : (i + 1) * 32, (i // 2) * 128 : (i // 2 + 1) * 128])
        d_mids.append(dot(blocks, d_logits).astype(BF16))
    heat_ref[...] = temper_grad
    slice_ref[...] = jnp.where(
        low_half, (slabs[0] + slabs[2]) + (slabs[4] + slabs[6]), (slabs[1] + slabs[3]) + (slabs[5] + slabs[7])
    )
    d_mid = jnp.concatenate(d_mids, axis=0)
    d_feat = jnp.concatenate(d_feats, axis=0)
    dmid_ref[...] = d_mid
    dfeat_ref[...] = d_feat
    out_grad = dot(jnp.concatenate(outs, axis=0), g_ref[...])
    in_grads = dot(normed_ref[...], jnp.concatenate([d_mid, d_feat], axis=0), ((0,), (1,)))
    halves = []
    for lanes in (slice(0, 128), slice(128, 256)):
        pieces = [out_grad[:, lanes], in_grads[:, :256][:, lanes], in_grads[:, 256:][:, lanes]]
        halves.append(jnp.concatenate([piece.reshape(PEERS, SHARE, 128) for piece in pieces], axis=1))
    first = lax.axis_index("c") == 0
    mine_ref[...] = jnp.where(first, halves[0], halves[1]).astype(BF16)
    other_ref[...] = jnp.where(first, halves[1], halves[0]).astype(BF16)


def norm_kernel(
    dmid_ref, dfeat_ref, wx_ref, wfx_ref, xhat_ref, rstd_ref, gain_ref, g_ref, slice_ref, heat_ref, token_ref, d_qkv_ref,
    feats_ref, small_ref,
):
    d_normed = dot(dmid_ref[...], wx_ref[...], ((0,), (1,))) + dot(dfeat_ref[...], wfx_ref[...], ((0,), (1,)))
    d_normed = d_normed.astype(BF16).astype(F32)
    xhat = xhat_ref[...]
    gain_grad = jnp.sum(d_normed * xhat, axis=0, keepdims=True)
    d_xhat = d_normed * gain_ref[...]
    d_x = rstd_ref[...] * (
        d_xhat
        - jnp.mean(d_xhat, axis=-1, keepdims=True)
        - xhat * jnp.mean(d_xhat * xhat, axis=-1, keepdims=True)
    )
    feats_ref[...] = (g_ref[...].astype(F32) + d_x).astype(BF16)
    qkv_grad = dot(token_ref[...], d_qkv_ref[...], ((0,), (0,)), HIGHEST)
    row = iota((8, 128), 0)
    vectors = jnp.where(row == 0, gain_grad[:, :128], jnp.where(row == 1, gain_grad[:, 128:], 0.0))
    small_ref[0:32, :] = slice_ref[...]
    small_ref[32:64, :] = jnp.concatenate([qkv_grad, jnp.zeros((DH, 32), F32)], axis=1)
    small_ref[64:72, :] = jnp.where(row == 2, heat_ref[...], vectors)
    small_ref[72:, :] = jnp.zeros((WIDTH - 72, 128), F32)


def add_kernel(a_ref, b_ref, small_ref, out_ref):
    total = a_ref[...].astype(F32) + b_ref[...].astype(F32)
    small = small_ref[...].reshape(PEERS, SHARE, 128)
    out_ref[...] = jnp.concatenate([total, small], axis=1).astype(BF16)


def sum_kernel(parts_ref, out_ref):
    total = jnp.sum(parts_ref[...].astype(F32), axis=0).astype(BF16)
    out_ref[...] = jnp.broadcast_to(total[None], out_ref.shape)


def finish_kernel(
    parts_ref,
    gain_hbm, in_x_hbm, in_fx_hbm, slice_hbm, temper_hbm, qkv_hbm, out_hbm,
    gain_ref, in_x_ref, in_fx_ref, slice_ref, temper_ref, qkv_ref, out_ref, sems,
):
    copies = []

    def leave(source, target):
        copies.append(pltpu.make_async_copy(source, target, sems.at[len(copies)]))
        copies[-1].start()

    for at, (ref, hbm) in enumerate(((out_ref, out_hbm), (in_x_ref, in_x_hbm), (in_fx_ref, in_fx_hbm))):
        for half in range(2):
            piece = parts_ref[half * PEERS : (half + 1) * PEERS].astype(F32)[:, at * SHARE : (at + 1) * SHARE]
            ref[:, half * 128 : (half + 1) * 128] = piece.reshape(WIDTH, 128)
        leave(ref, hbm)
    small = parts_ref[:PEERS].astype(F32)[:, 3 * SHARE :] + parts_ref[PEERS:].astype(F32)[:, 3 * SHARE :]
    small = small.reshape(WIDTH, 128)
    slices = small[0:32]
    slice_ref[...] = slices[:, :64] + slices[:, 64:]
    leave(slice_ref, slice_hbm)
    qkv_ref[...] = small[32:64, :96]
    leave(qkv_ref, qkv_hbm)
    gain_ref[:, :128] = small[64:65]
    gain_ref[:, 128:] = small[65:66]
    leave(gain_ref, gain_hbm)
    temper_ref[...] = small[66:67, :8]
    leave(temper_ref, temper_hbm)
    for copy in copies:
        copy.wait()


def call(kernel, name, inputs, outputs, scalars=0, far_in=False, far_out=False, scratch=(), cost=None):
    single = not isinstance(outputs, (list, tuple))
    in_spec = pl.BlockSpec(memory_space=pltpu.HBM if far_in else pltpu.VMEM)
    out_spec = pl.BlockSpec(memory_space=pltpu.HBM if far_out else pltpu.VMEM)
    return pl.pallas_call(
        kernel,
        name=name,
        out_shape=outputs,
        in_specs=[pl.BlockSpec(memory_space=pltpu.SMEM)] * scalars + [in_spec] * (len(inputs) - scalars),
        out_specs=out_spec if single else [out_spec] * len(outputs),
        scratch_shapes=scratch,
        compiler_params=pltpu.CompilerParams(vmem_limit_bytes=48 * 1024 * 1024),
        cost_estimate=cost,
    )(*inputs)


def shape(dims, dtype=BF16):
    return jax.ShapeDtypeStruct(dims, dtype)


def shards(
    node_feats, cotangent, mesh_of_block, block_rows, ln_gain, w_in_x, w_in_fx, w_slice, temper, w_qkv, w_out
):
    x = node_feats.reshape(ROWS, WIDTH)
    cot = cotangent.reshape(ROWS, WIDTH)
    gain = ln_gain.reshape(1, WIDTH)
    wide = shape((ROWS, WIDTH))
    packets = shape((2 * HEADS, 40, 128))
    owned = shape((OWNERS, 40, 128))
    tall = shape((2 * WIDTH, ROWS), F32)
    flat = shape((WIDTH, ROWS))
    inputs = (x, gain, w_in_x, w_in_fx, w_slice, temper.reshape(1, HEADS), cot, w_out)
    far = [pltpu.with_memory_space_constraint(a, pltpu.HBM) for a in inputs]
    scratch = [pltpu.VMEM(a.shape, a.dtype) for a in (x, w_slice, inputs[5], cot, w_out)]
    scratch.append(pltpu.SemaphoreType.DMA((len(far),)))
    send, normed, mid, feat, sw, d_out, scaled, weights, xhat, rstd, gains, wx, wfx, g, diagonal, heat = call(
        front_kernel,
        "front",
        (block_rows, mesh_of_block, *far),
        [
            packets, wide, flat, wide, shape((2 * WIDTH, ROWS)), wide,
            tall, tall, shape((ROWS, WIDTH), F32), shape((ROWS, 1), F32),
            shape((1, WIDTH), F32), shape((WIDTH, WIDTH)), shape((WIDTH, WIDTH)), wide,
            shape((128, 256)), shape((2 * WIDTH, 1), F32),
        ],
        scalars=2,
        far_in=True,
        scratch=scratch,
    )
    blocks = lax.all_to_all(send, ("y", "c", "zl"), 0, 0)
    dense = call(dense_kernel, "dense", (blocks,), owned)
    sums = lax.all_to_all(dense, "zh", 0, 0)
    answer, token, d_qkv = call(
        attend_kernel,
        "attend",
        (sums, w_qkv),
        [owned, shape((SLICES, DH), F32), shape((SLICES, 3 * DH), F32)],
    )
    meshes = lax.all_to_all(answer, "zh", 0, 0)
    chosen = call(choose_kernel, "choose", (blocks, meshes), packets)
    tokens = lax.all_to_all(chosen, ("y", "c", "zl"), 0, 0)
    share = shape((PEERS, 4 * SHARE, 128))
    big = shape((PEERS, 3 * SHARE, 128))
    mine, other, d_mid, d_feat, slice_grad, temper_grad = call(
        back_kernel,
        "back",
        (normed, mid, feat, sw, d_out, scaled, weights, g, diagonal, heat, tokens),
        [big, big, flat, flat, shape((DH, 128), F32), shape((1, 128), F32)],
    )
    other = lax.ppermute(other, "c", [(0, 1), (1, 0)])
    feats_grad, small = call(
        norm_kernel,
        "norm",
        (d_mid, d_feat, wx, wfx, xhat, rstd, gains, g, slice_grad, temper_grad, token, d_qkv),
        [wide, shape((WIDTH, 128), F32)],
        cost=pl.CostEstimate(flops=4 * ROWS * WIDTH * WIDTH, bytes_accessed=4 * 1024 * 1024, transcendentals=0),
    )
    across = ("y", "zl", "x")
    parts = call(add_kernel, "add_pair", (mine, other, small), share)
    parts = lax.all_to_all(parts, across, 0, 0)
    parts = call(sum_kernel, "sum_peers", (parts,), shape((OWNERS, 4 * SHARE, 128)))
    parts = lax.all_to_all(parts, "zh", 0, 0)
    parts = call(sum_kernel, "sum_z", (parts,), share)
    parts = lax.all_to_all(parts, across, 0, 0)
    parts = lax.all_gather(parts, "c", axis=0, tiled=True)
    square = shape((WIDTH, WIDTH), F32)
    results = [
        shape((1, WIDTH), F32), square, square, shape((DH, SLICES), F32),
        shape((1, HEADS), F32), shape((DH, 3 * DH), F32), square,
    ]
    gain_grad, in_x_grad, in_fx_grad, slice_grad, temper_grad, qkv_grad, out_grad = call(
        finish_kernel,
        "finish",
        (parts,),
        results,
        far_out=True,
        scratch=[pltpu.VMEM(r.shape, r.dtype) for r in results] + [pltpu.SemaphoreType.DMA((len(results),))],
    )
    return (
        feats_grad.reshape(1, 1, ROWS, WIDTH),
        gain_grad.reshape(WIDTH),
        in_x_grad,
        in_fx_grad,
        slice_grad,
        temper_grad.reshape(HEADS),
        qkv_grad,
        out_grad,
    )


def solution(mesh):
    groups = mesh.shape["dp"]
    devices = mesh.devices.reshape(4, OWNERS, 2, 2, groups)
    grid = Mesh(devices, ("y", "zh", "zl", "c", "x"))
    node = ("y", "zh", "zl", "c")
    blocks = P("x", node, None, None)
    scalars = P("x", node)
    return jax.shard_map(
        shards,
        mesh=grid,
        in_specs=(blocks, blocks, scalars, scalars) + (P(),) * 7,
        out_specs=(blocks,) + (P(),) * 7,
        check_vma=False,
    )
```

```python
import math

import jax
import jax.numpy as jnp
from jax import lax
from jax.experimental import pallas as pl
from jax.experimental.pallas import tpu as pltpu
from jax.sharding import Mesh
from jax.sharding import PartitionSpec as P

EPS_NORM = 1e-05
EPS_MASS = 1e-05
HEADS = 8
DH = 32
SLICES = 64
WIDTH = 256
ROWS = 512
OWNERS = 8
PEERS = 32
SHARE = 8
F32 = jnp.float32
BF16 = jnp.bfloat16
HIGHEST = lax.Precision.HIGHEST


def iota(shape, dim):
    return lax.broadcasted_iota(jnp.int32, shape, dim)


def dot(a, b, dims=((1,), (0,)), precision=None):
    return lax.dot_general(a, b, (dims, ((), ())), precision=precision, preferred_element_type=F32)


def four_blocks(w_slice):
    two = jnp.concatenate([w_slice, w_slice], axis=1)
    four = jnp.concatenate([two, two], axis=1)
    tall = jnp.concatenate([four] * 4, axis=0)
    same = (iota((128, 256), 0) >> 5) == (iota((128, 256), 1) >> 6)
    return jnp.where(same, tall, 0.0).astype(BF16)


def fold_matrix():
    return ((iota((128, 128), 0) & 31) == (iota((128, 128), 1) & 31)).astype(F32).astype(BF16)


def quarter_mask(rows):
    return ((iota((rows, 128), 0) & 63) >> 4) == (iota((rows, 128), 1) >> 5)


def pack_rows(tiled):
    rows = tiled.shape[0]
    kept = jnp.where(quarter_mask(rows), tiled, 0.0)
    return jnp.sum(kept.reshape(rows // 64, 4, 16, 128), axis=1)


def spread_rows(packed):
    heads = packed.shape[0]
    tall = jnp.broadcast_to(packed[:, None], (heads, 4, 16, 128)).reshape(heads * 64, 128)
    return jnp.where(quarter_mask(heads * 64), tall, 0.0)


def temper_column(temper, group):
    head = iota((256, 1), 0) >> 6
    column = jnp.zeros((256, 1), F32)
    for i in range(4):
        column = jnp.where(head == i, temper[:, 4 * group + i : 4 * group + i + 1], column)
    return column


def head_sums(values):
    rows, nodes = values.shape
    sums = jnp.sum(values.reshape(rows // 64, 64, nodes), axis=1, keepdims=True)
    return jnp.broadcast_to(sums, (rows // 64, 64, nodes)).reshape(rows, nodes)


def eye_mask():
    return iota((SLICES, 128), 0) == iota((SLICES, 128), 1)


def column_to_row(column):
    return jnp.sum(jnp.where(eye_mask(), column, 0.0), axis=0, keepdims=True)


def row_to_column(row):
    return jnp.sum(jnp.where(eye_mask(), row, 0.0), axis=1, keepdims=True)


def normalise(x):
    xf = x.astype(F32)
    mean = jnp.mean(xf, axis=-1, keepdims=True)
    centered = xf - mean
    var = jnp.mean(centered * centered, axis=-1, keepdims=True)
    rstd = lax.rsqrt(var + EPS_NORM)
    return centered * rstd, rstd


def front_kernel(
    rows_ref, mesh_ref, x_hbm, gain_hbm, wx_hbm, wfx_hbm, slice_hbm, temper_hbm, cot_hbm, wout_hbm,
    send_ref, normed_ref, mid_ref, feat_ref, sw_ref, dout_ref, scaled_ref, weights_ref, xhat_ref, rstd_ref,
    gain_ref, wx_ref, wfx_ref, g_ref, blocks_ref, temper_ref,
    x_ref, slice_ref, heat_ref, cot_ref, wout_ref, sems,
):
    sources = (x_hbm, gain_hbm, wx_hbm, wfx_hbm, slice_hbm, temper_hbm, cot_hbm, wout_hbm)
    targets = (x_ref, gain_ref, wx_ref, wfx_ref, slice_ref, heat_ref, cot_ref, wout_ref)
    copies = [pltpu.make_async_copy(a, b, sems.at[i]) for i, (a, b) in enumerate(zip(sources, targets))]
    for copy in copies:
        copy.start()
    copies[0].wait()
    xhat, rstd = normalise(x_ref[...])
    xhat_ref[...] = xhat
    rstd_ref[...] = rstd
    copies[1].wait()
    normed = (xhat * gain_ref[...]).astype(BF16)
    normed_ref[...] = normed
    copies[2].wait()
    mid = dot(wx_ref[...], normed, ((0,), (1,))).astype(BF16)
    copies[3].wait()
    feat = dot(normed, wfx_ref[...]).astype(BF16)
    mid_ref[...] = mid
    feat_ref[...] = feat
    copies[4].wait()
    blocks = four_blocks(slice_ref[...])
    blocks_ref[...] = blocks
    copies[5].wait()
    heat = heat_ref[...]
    copies[6].wait()
    g_b = jnp.where(iota((ROWS, 1), 0) < rows_ref[0, 0], cot_ref[...].astype(F32), 0.0).astype(BF16)
    g_ref[...] = g_b
    copies[7].wait()
    d_out = dot(g_b, wout_ref[...], ((1,), (1,))).astype(BF16)
    dout_ref[...] = d_out
    fold = fold_matrix()
    diagonal = (iota((256, 256), 0) >> 6) == ((iota((256, 256), 1) & 127) >> 5)
    valid = (iota((1, ROWS), 1) < rows_ref[0, 0]).astype(F32)
    tables, grads, masses = [], [], []
    for group in range(2):
        lanes = slice(group * 128, (group + 1) * 128)
        wide = slice(group * 256, (group + 1) * 256)
        inv_temper = 1.0 / temper_column(heat, group)
        temper_ref[wide, :] = inv_temper
        scaled = dot(blocks, mid[lanes], ((0,), (0,))) * inv_temper
        expo = jnp.exp(scaled)
        weights = expo / head_sums(expo) * valid
        sw = weights.astype(BF16)
        scaled_ref[wide, :] = scaled
        weights_ref[wide, :] = weights
        sw_ref[wide, :] = sw
        both = jnp.concatenate([feat[:, lanes], d_out[:, lanes]], axis=1)
        full = jnp.where(diagonal, dot(sw, both), 0.0).astype(BF16)
        tables.append(pack_rows(dot(full[:, :128], fold)))
        grads.append(pack_rows(dot(full[:, 128:], fold)))
        mass = jnp.sum(weights, axis=1, keepdims=True)
        masses += [column_to_row(mass[64 * i : 64 * i + 64]) for i in range(4)]
    row = iota((8, 128), 0)
    mesh = mesh_ref[0, 0]
    number = jnp.where(row == 1, ((mesh >> 1) + 1).astype(F32), 0.0)
    tails = [jnp.where(row == 0, mass, number)[None] for mass in masses]
    packed = [jnp.concatenate(tables, axis=0), jnp.concatenate(grads, axis=0), jnp.concatenate(tails, axis=0)]
    packed = jnp.concatenate(packed, axis=1)
    odd = (mesh & 1).astype(F32)
    send_ref[...] = jnp.concatenate([packed * (1.0 - odd), packed * odd], axis=0).astype(BF16)


def dense_kernel(blocks_ref, out_ref):
    blocks = blocks_ref[...].astype(F32)
    numbers = blocks[:, 33:34, :]
    for k in range(OWNERS):
        out_ref[k] = jnp.sum(jnp.where(numbers == float(k + 1), blocks, 0.0), axis=0).astype(BF16)


def attend_kernel(sums_ref, qkv_ref, out_ref, token_ref, d_qkv_ref):
    sums = jnp.sum(sums_ref[...].astype(F32), axis=0)
    w_qkv = qkv_ref[...]
    mass = row_to_column(sums[32:33, :])
    inv = 1.0 / (mass + EPS_MASS)

    def unfold(spread):
        return (spread[:, 0:32] + spread[:, 32:64]) + (spread[:, 64:96] + spread[:, 96:128])

    token = unfold(spread_rows(sums[None, 0:16, :])) * inv
    d_mixed = unfold(spread_rows(sums[None, 16:32, :])).astype(BF16).astype(F32)
    scale = 1.0 / math.sqrt(DH)
    query = dot(token, w_qkv[:, 0:32], precision=HIGHEST)
    keys = dot(token, w_qkv[:, 32:64], precision=HIGHEST)
    values = dot(token, w_qkv[:, 64:96], precision=HIGHEST)
    expo = jnp.exp(dot(query, keys, ((1,), (1,)), HIGHEST) * scale)
    probs = expo / jnp.sum(expo, axis=-1, keepdims=True)
    mixed = dot(probs, values, precision=HIGHEST)
    d_values = dot(probs, d_mixed, ((0,), (0,)), HIGHEST)
    d_probs = dot(d_mixed, values, ((1,), (1,)), HIGHEST)
    d_scores = probs * (d_probs - jnp.sum(probs * d_probs, axis=-1, keepdims=True)) * scale
    d_query = dot(d_scores, keys, precision=HIGHEST)
    d_keys = dot(d_scores, query, ((0,), (0,)), HIGHEST)
    d_qkv = jnp.concatenate([d_query, d_keys, d_values], axis=1)
    token_ref[...] = token
    d_qkv_ref[...] = d_qkv
    d_token = dot(d_qkv, w_qkv, ((1,), (1,)), HIGHEST)
    d_table = d_token * inv
    d_mass = -jnp.sum(d_token * token, axis=1, keepdims=True) * inv

    def pack(values):
        return pack_rows(jnp.concatenate([values] * 4, axis=1))[0]

    tail = jnp.where(iota((8, 128), 0) == 0, column_to_row(d_mass), 0.0)
    packed = jnp.concatenate([pack(mixed), pack(d_table), tail], axis=0).astype(BF16)
    out_ref[...] = jnp.broadcast_to(packed[None], (OWNERS, 40, 128))


def choose_kernel(blocks_ref, meshes_ref, out_ref):
    numbers = blocks_ref[...].astype(F32)[:, 33:34, :]
    meshes = meshes_ref[...].astype(F32)
    for b in range(2 * HEADS):
        chosen = jnp.zeros((40, 128), F32)
        for k in range(OWNERS):
            chosen = jnp.where(numbers[b] == float(k + 1), meshes[k], chosen)
        out_ref[b] = chosen.astype(BF16)


def back_kernel(
    normed_ref, mid_ref, feat_ref, sw_ref, dout_ref, scaled_ref, weights_ref, g_ref, blocks_ref, temper_ref, tokens_ref,
    mine_ref, other_ref, dmid_ref, dfeat_ref, slice_ref, heat_ref,
):
    tokens = jnp.sum(tokens_ref[...].astype(F32).reshape(2, HEADS, 40, 128), axis=0)
    blocks = blocks_ref[...]
    fold = fold_matrix()
    diagonal = (iota((256, 128), 0) >> 6) == (iota((256, 128), 1) >> 5)
    low_half = iota((1, 128), 1) < 64
    feat = feat_ref[...]
    d_out = dout_ref[...]
    outs, d_mids, d_feats, slabs = [], [], [], []
    temper_grad = jnp.zeros((1, 128), F32)
    lane = iota((1, 128), 1)

    def block_of(packed):
        tiled = dot(spread_rows(packed).astype(BF16), fold)
        return jnp.where(diagonal, tiled, 0.0).astype(BF16)

    for group in range(2):
        lanes = slice(group * 128, (group + 1) * 128)
        wide = slice(group * 256, (group + 1) * 256)
        heads = tokens[4 * group : 4 * group + 4]
        chosen = jnp.concatenate([block_of(heads[:, 0:16]), block_of(heads[:, 16:32])], axis=1)
        d_mass = jnp.concatenate([row_to_column(heads[i, 32:33, :]) for i in range(4)], axis=0)
        pair = dot(chosen, sw_ref[wide, :], ((0,), (0,)))
        outs.append(pair[:128].astype(BF16))
        d_feats.append(pair[128:].astype(BF16))
        left = jnp.concatenate([d_out[:, lanes], feat[:, lanes]], axis=1)
        d_sw = dot(chosen, left, ((1,), (1,))).astype(BF16).astype(F32)
        d_weights = d_sw + d_mass
        inv_temper = temper_ref[wide, :]
        weights = weights_ref[wide, :]
        d_scaled = weights * (d_weights - head_sums(weights * d_weights))
        products = jnp.sum((d_scaled * scaled_ref[wide, :]).reshape(4, SLICES, ROWS), axis=1)
        totals = jnp.sum(products, axis=1, keepdims=True)
        for i in range(4):
            total = -totals[i : i + 1] * inv_temper[64 * i : 64 * i + 1]
            temper_grad = jnp.where(lane == 4 * group + i, total, temper_grad)
        d_logits = (d_scaled * inv_temper).astype(BF16)
        d_block = dot(mid_ref[lanes, :], d_logits, ((1,), (1,)))
        for i in range(4):
            slabs.append(d_block[i * 32 : (i + 1) * 32, (i // 2) * 128 : (i // 2 + 1) * 128])
        d_mids.append(dot(blocks, d_logits).astype(BF16))
    heat_ref[...] = temper_grad
    slice_ref[...] = jnp.where(
        low_half, (slabs[0] + slabs[2]) + (slabs[4] + slabs[6]), (slabs[1] + slabs[3]) + (slabs[5] + slabs[7])
    )
    d_mid = jnp.concatenate(d_mids, axis=0)
    d_feat = jnp.concatenate(d_feats, axis=0)
    dmid_ref[...] = d_mid
    dfeat_ref[...] = d_feat
    out_grad = dot(jnp.concatenate(outs, axis=0), g_ref[...])
    in_grads = dot(normed_ref[...], jnp.concatenate([d_mid, d_feat], axis=0), ((0,), (1,)))
    halves = []
    for lanes in (slice(0, 128), slice(128, 256)):
        pieces = [out_grad[:, lanes], in_grads[:, :256][:, lanes], in_grads[:, 256:][:, lanes]]
        halves.append(jnp.concatenate([piece.reshape(PEERS, SHARE, 128) for piece in pieces], axis=1))
    first = lax.axis_index("c") == 0
    mine_ref[...] = jnp.where(first, halves[0], halves[1]).astype(BF16)
    other_ref[...] = jnp.where(first, halves[1], halves[0]).astype(BF16)


def norm_kernel(
    dmid_ref, dfeat_ref, wx_ref, wfx_ref, xhat_ref, rstd_ref, gain_ref, g_ref, slice_ref, heat_ref, token_ref, d_qkv_ref,
    feats_ref, small_ref,
):
    d_normed = dot(dmid_ref[...], wx_ref[...], ((0,), (1,))) + dot(dfeat_ref[...], wfx_ref[...], ((0,), (1,)))
    d_normed = d_normed.astype(BF16).astype(F32)
    xhat = xhat_ref[...]
    gain_grad = jnp.sum(d_normed * xhat, axis=0, keepdims=True)
    d_xhat = d_normed * gain_ref[...]
    d_x = rstd_ref[...] * (
        d_xhat
        - jnp.mean(d_xhat, axis=-1, keepdims=True)
        - xhat * jnp.mean(d_xhat * xhat, axis=-1, keepdims=True)
    )
    feats_ref[...] = (g_ref[...].astype(F32) + d_x).astype(BF16)
    qkv_grad = dot(token_ref[...], d_qkv_ref[...], ((0,), (0,)), HIGHEST)
    row = iota((8, 128), 0)
    vectors = jnp.where(row == 0, gain_grad[:, :128], jnp.where(row == 1, gain_grad[:, 128:], 0.0))
    small_ref[0:32, :] = slice_ref[...]
    small_ref[32:64, :] = jnp.concatenate([qkv_grad, jnp.zeros((DH, 32), F32)], axis=1)
    small_ref[64:72, :] = jnp.where(row == 2, heat_ref[...], vectors)
    small_ref[72:, :] = jnp.zeros((WIDTH - 72, 128), F32)


def add_kernel(a_ref, b_ref, small_ref, out_ref):
    total = a_ref[...].astype(F32) + b_ref[...].astype(F32)
    small = small_ref[...].reshape(PEERS, SHARE, 128)
    out_ref[...] = jnp.concatenate([total, small], axis=1).astype(BF16)


def sum_kernel(parts_ref, out_ref):
    total = jnp.sum(parts_ref[...].astype(F32), axis=0).astype(BF16)
    out_ref[...] = jnp.broadcast_to(total[None], out_ref.shape)


def finish_kernel(
    parts_ref,
    gain_hbm, in_x_hbm, in_fx_hbm, slice_hbm, temper_hbm, qkv_hbm, out_hbm,
    gain_ref, in_x_ref, in_fx_ref, slice_ref, temper_ref, qkv_ref, out_ref, sems,
):
    copies = []

    def leave(source, target):
        copies.append(pltpu.make_async_copy(source, target, sems.at[len(copies)]))
        copies[-1].start()

    for at, (ref, hbm) in enumerate(((out_ref, out_hbm), (in_x_ref, in_x_hbm), (in_fx_ref, in_fx_hbm))):
        for half in range(2):
            piece = parts_ref[half * PEERS : (half + 1) * PEERS].astype(F32)[:, at * SHARE : (at + 1) * SHARE]
            ref[:, half * 128 : (half + 1) * 128] = piece.reshape(WIDTH, 128)
        leave(ref, hbm)
    small = parts_ref[:PEERS].astype(F32)[:, 3 * SHARE :] + parts_ref[PEERS:].astype(F32)[:, 3 * SHARE :]
    small = small.reshape(WIDTH, 128)
    slices = small[0:32]
    slice_ref[...] = slices[:, :64] + slices[:, 64:]
    leave(slice_ref, slice_hbm)
    qkv_ref[...] = small[32:64, :96]
    leave(qkv_ref, qkv_hbm)
    gain_ref[:, :128] = small[64:65]
    gain_ref[:, 128:] = small[65:66]
    leave(gain_ref, gain_hbm)
    temper_ref[...] = small[66:67, :8]
    leave(temper_ref, temper_hbm)
    for copy in copies:
        copy.wait()


def call(kernel, name, inputs, outputs, scalars=0, far_in=False, far_out=False, scratch=(), cost=None):
    single = not isinstance(outputs, (list, tuple))
    in_spec = pl.BlockSpec(memory_space=pltpu.HBM if far_in else pltpu.VMEM)
    out_spec = pl.BlockSpec(memory_space=pltpu.HBM if far_out else pltpu.VMEM)
    return pl.pallas_call(
        kernel,
        name=name,
        out_shape=outputs,
        in_specs=[pl.BlockSpec(memory_space=pltpu.SMEM)] * scalars + [in_spec] * (len(inputs) - scalars),
        out_specs=out_spec if single else [out_spec] * len(outputs),
        scratch_shapes=scratch,
        compiler_params=pltpu.CompilerParams(vmem_limit_bytes=48 * 1024 * 1024),
        cost_estimate=cost,
    )(*inputs)


def shape(dims, dtype=BF16):
    return jax.ShapeDtypeStruct(dims, dtype)


def shards(
    node_feats, cotangent, mesh_of_block, block_rows, ln_gain, w_in_x, w_in_fx, w_slice, temper, w_qkv, w_out
):
    x = node_feats.reshape(ROWS, WIDTH)
    cot = cotangent.reshape(ROWS, WIDTH)
    gain = ln_gain.reshape(1, WIDTH)
    wide = shape((ROWS, WIDTH))
    packets = shape((2 * HEADS, 40, 128))
    owned = shape((OWNERS, 40, 128))
    tall = shape((2 * WIDTH, ROWS), F32)
    flat = shape((WIDTH, ROWS))
    inputs = (x, gain, w_in_x, w_in_fx, w_slice, temper.reshape(1, HEADS), cot, w_out)
    far = [pltpu.with_memory_space_constraint(a, pltpu.HBM) for a in inputs]
    scratch = [pltpu.VMEM(a.shape, a.dtype) for a in (x, w_slice, inputs[5], cot, w_out)]
    scratch.append(pltpu.SemaphoreType.DMA((len(far),)))
    send, normed, mid, feat, sw, d_out, scaled, weights, xhat, rstd, gains, wx, wfx, g, diagonal, heat = call(
        front_kernel,
        "front",
        (block_rows, mesh_of_block, *far),
        [
            packets, wide, flat, wide, shape((2 * WIDTH, ROWS)), wide,
            tall, tall, shape((ROWS, WIDTH), F32), shape((ROWS, 1), F32),
            shape((1, WIDTH), F32), shape((WIDTH, WIDTH)), shape((WIDTH, WIDTH)), wide,
            shape((128, 256)), shape((2 * WIDTH, 1), F32),
        ],
        scalars=2,
        far_in=True,
        scratch=scratch,
    )
    blocks = lax.all_to_all(send, ("zl", "y", "c"), 0, 0)
    dense = call(dense_kernel, "dense", (blocks,), owned)
    sums = lax.all_to_all(dense, ("zb", "zc", "za"), 0, 0)
    answer, token, d_qkv = call(
        attend_kernel,
        "attend",
        (sums, w_qkv),
        [owned, shape((SLICES, DH), F32), shape((SLICES, 3 * DH), F32)],
    )
    meshes = lax.all_to_all(answer, ("zb", "zc", "za"), 0, 0)
    chosen = call(choose_kernel, "choose", (blocks, meshes), packets)
    tokens = lax.all_to_all(chosen, ("zl", "y", "c"), 0, 0)
    share = shape((PEERS, 4 * SHARE, 128))
    big = shape((PEERS, 3 * SHARE, 128))
    mine, other, d_mid, d_feat, slice_grad, temper_grad = call(
        back_kernel,
        "back",
        (normed, mid, feat, sw, d_out, scaled, weights, g, diagonal, heat, tokens),
        [big, big, flat, flat, shape((DH, 128), F32), shape((1, 128), F32)],
    )
    other = lax.ppermute(other, "c", [(0, 1), (1, 0)])
    feats_grad, small = call(
        norm_kernel,
        "norm",
        (d_mid, d_feat, wx, wfx, xhat, rstd, gains, g, slice_grad, temper_grad, token, d_qkv),
        [wide, shape((WIDTH, 128), F32)],
        cost=pl.CostEstimate(flops=4 * ROWS * WIDTH * WIDTH, bytes_accessed=4 * 1024 * 1024, transcendentals=0),
    )
    across = ("y", "zl", "x")
    parts = call(add_kernel, "add_pair", (mine, other, small), share)
    parts = lax.all_to_all(parts, across, 0, 0)
    parts = call(sum_kernel, "sum_peers", (parts,), shape((OWNERS, 4 * SHARE, 128)))
    parts = lax.all_to_all(parts, ("zb", "zc", "za"), 0, 0)
    parts = call(sum_kernel, "sum_z", (parts,), share)
    parts = lax.all_to_all(parts, across, 0, 0)
    parts = lax.all_gather(parts, "c", axis=0, tiled=True)
    square = shape((WIDTH, WIDTH), F32)
    results = [
        shape((1, WIDTH), F32), square, square, shape((DH, SLICES), F32),
        shape((1, HEADS), F32), shape((DH, 3 * DH), F32), square,
    ]
    gain_grad, in_x_grad, in_fx_grad, slice_grad, temper_grad, qkv_grad, out_grad = call(
        finish_kernel,
        "finish",
        (parts,),
        results,
        far_out=True,
        scratch=[pltpu.VMEM(r.shape, r.dtype) for r in results] + [pltpu.SemaphoreType.DMA((len(results),))],
    )
    return (
        feats_grad.reshape(1, 1, ROWS, WIDTH),
        gain_grad.reshape(WIDTH),
        in_x_grad,
        in_fx_grad,
        slice_grad,
        temper_grad.reshape(HEADS),
        qkv_grad,
        out_grad,
    )


def solution(mesh):
    groups = mesh.shape["dp"]
    devices = mesh.devices.reshape(4, 2, 2, 2, 2, 2, groups)
    grid = Mesh(devices, ("y", "za", "zb", "zc", "zl", "c", "x"))
    node = ("y", "za", "zb", "zc", "zl", "c")
    blocks = P("x", node, None, None)
    scalars = P("x", node)
    return jax.shard_map(
        shards,
        mesh=grid,
        in_specs=(blocks, blocks, scalars, scalars) + (P(),) * 7,
        out_specs=(blocks,) + (P(),) * 7,
        check_vma=False,
    )
```

```python
import math

import jax
import jax.numpy as jnp
from jax import lax
from jax.experimental import pallas as pl
from jax.experimental.pallas import tpu as pltpu
from jax.sharding import Mesh
from jax.sharding import PartitionSpec as P

EPS_NORM = 1e-05
EPS_MASS = 1e-05
HEADS = 8
DH = 32
SLICES = 64
WIDTH = 256
ROWS = 512
OWNERS = 8
PEERS = 32
SHARE = 8
F32 = jnp.float32
BF16 = jnp.bfloat16
HIGHEST = lax.Precision.HIGHEST


def iota(shape, dim):
    return lax.broadcasted_iota(jnp.int32, shape, dim)


def dot(a, b, dims=((1,), (0,)), precision=None):
    return lax.dot_general(a, b, (dims, ((), ())), precision=precision, preferred_element_type=F32)


def four_blocks(w_slice):
    two = jnp.concatenate([w_slice, w_slice], axis=1)
    four = jnp.concatenate([two, two], axis=1)
    tall = jnp.concatenate([four] * 4, axis=0)
    same = (iota((128, 256), 0) >> 5) == (iota((128, 256), 1) >> 6)
    return jnp.where(same, tall, 0.0).astype(BF16)


def fold_matrix():
    return ((iota((128, 128), 0) & 31) == (iota((128, 128), 1) & 31)).astype(F32).astype(BF16)


def quarter_mask(rows):
    return ((iota((rows, 128), 0) & 63) >> 4) == (iota((rows, 128), 1) >> 5)


def pack_rows(tiled):
    rows = tiled.shape[0]
    kept = jnp.where(quarter_mask(rows), tiled, 0.0)
    return jnp.sum(kept.reshape(rows // 64, 4, 16, 128), axis=1)


def spread_rows(packed):
    heads = packed.shape[0]
    tall = jnp.broadcast_to(packed[:, None], (heads, 4, 16, 128)).reshape(heads * 64, 128)
    return jnp.where(quarter_mask(heads * 64), tall, 0.0)


def temper_column(temper, group):
    head = iota((256, 1), 0) >> 6
    column = jnp.zeros((256, 1), F32)
    for i in range(4):
        column = jnp.where(head == i, temper[:, 4 * group + i : 4 * group + i + 1], column)
    return column


def head_sums(values):
    rows, nodes = values.shape
    sums = jnp.sum(values.reshape(rows // 64, 64, nodes), axis=1, keepdims=True)
    return jnp.broadcast_to(sums, (rows // 64, 64, nodes)).reshape(rows, nodes)


def eye_mask():
    return iota((SLICES, 128), 0) == iota((SLICES, 128), 1)


def column_to_row(column):
    return jnp.sum(jnp.where(eye_mask(), column, 0.0), axis=0, keepdims=True)


def row_to_column(row):
    return jnp.sum(jnp.where(eye_mask(), row, 0.0), axis=1, keepdims=True)


def low_part(values):
    return values - values.astype(BF16).astype(F32)


def normalise(x):
    xf = x.astype(F32)
    mean = jnp.mean(xf, axis=-1, keepdims=True)
    centered = xf - mean
    var = jnp.mean(centered * centered, axis=-1, keepdims=True)
    rstd = lax.rsqrt(var + EPS_NORM)
    return centered * rstd, rstd


def front_kernel(
    rows_ref, mesh_ref, x_hbm, gain_hbm, wx_hbm, wfx_hbm, slice_hbm, temper_hbm, cot_hbm, wout_hbm,
    send_ref, normed_ref, mid_ref, feat_ref, sw_ref, dout_ref, scaled_ref, weights_ref, xhat_ref, rstd_ref,
    gain_ref, wx_ref, wfx_ref, g_ref, blocks_ref, temper_ref,
    x_ref, slice_ref, heat_ref, cot_ref, wout_ref, sems,
):
    sources = (x_hbm, gain_hbm, wx_hbm, wfx_hbm, slice_hbm, temper_hbm, cot_hbm, wout_hbm)
    targets = (x_ref, gain_ref, wx_ref, wfx_ref, slice_ref, heat_ref, cot_ref, wout_ref)
    copies = [pltpu.make_async_copy(a, b, sems.at[i]) for i, (a, b) in enumerate(zip(sources, targets))]
    for copy in copies:
        copy.start()
    copies[0].wait()
    xhat, rstd = normalise(x_ref[...])
    xhat_ref[...] = xhat
    rstd_ref[...] = rstd
    copies[1].wait()
    normed = (xhat * gain_ref[...]).astype(BF16)
    normed_ref[...] = normed
    copies[2].wait()
    mid = dot(wx_ref[...], normed, ((0,), (1,))).astype(BF16)
    copies[3].wait()
    feat = dot(normed, wfx_ref[...]).astype(BF16)
    mid_ref[...] = mid
    feat_ref[...] = feat
    copies[4].wait()
    blocks = four_blocks(slice_ref[...])
    blocks_ref[...] = blocks
    copies[5].wait()
    heat = heat_ref[...]
    copies[6].wait()
    g_b = jnp.where(iota((ROWS, 1), 0) < rows_ref[0, 0], cot_ref[...].astype(F32), 0.0).astype(BF16)
    g_ref[...] = g_b
    copies[7].wait()
    d_out = dot(g_b, wout_ref[...], ((1,), (1,))).astype(BF16)
    dout_ref[...] = d_out
    fold = fold_matrix()
    diagonal = (iota((256, 256), 0) >> 6) == ((iota((256, 256), 1) & 127) >> 5)
    valid = (iota((1, ROWS), 1) < rows_ref[0, 0]).astype(F32)
    tables, grads, masses = [], [], []
    for group in range(2):
        lanes = slice(group * 128, (group + 1) * 128)
        wide = slice(group * 256, (group + 1) * 256)
        inv_temper = 1.0 / temper_column(heat, group)
        temper_ref[wide, :] = inv_temper
        scaled = dot(blocks, mid[lanes], ((0,), (0,))) * inv_temper
        expo = jnp.exp(scaled)
        weights = expo / head_sums(expo) * valid
        sw = weights.astype(BF16)
        scaled_ref[wide, :] = scaled
        weights_ref[wide, :] = weights
        sw_ref[wide, :] = sw
        both = jnp.concatenate([feat[:, lanes], d_out[:, lanes]], axis=1)
        full = jnp.where(diagonal, dot(sw, both), 0.0).astype(BF16)
        tables.append(pack_rows(dot(full[:, :128], fold)))
        grads.append(pack_rows(dot(full[:, 128:], fold)))
        mass = jnp.sum(weights, axis=1, keepdims=True)
        masses += [column_to_row(mass[64 * i : 64 * i + 64]) for i in range(4)]
    row = iota((8, 128), 0)
    mesh = mesh_ref[0, 0]
    number = jnp.where(row == 1, ((mesh >> 1) + 1).astype(F32), 0.0)
    tails = [jnp.where(row == 0, mass, jnp.where(row == 2, low_part(mass), number))[None] for mass in masses]
    packed = [jnp.concatenate(tables, axis=0), jnp.concatenate(grads, axis=0), jnp.concatenate(tails, axis=0)]
    packed = jnp.concatenate(packed, axis=1)
    odd = (mesh & 1).astype(F32)
    send_ref[...] = jnp.concatenate([packed * (1.0 - odd), packed * odd], axis=0).astype(BF16)


def dense_kernel(blocks_ref, out_ref):
    blocks = blocks_ref[...].astype(F32)
    numbers = blocks[:, 33:34, :]
    row = iota((40, 128), 0)
    for k in range(OWNERS):
        total = jnp.sum(jnp.where(numbers == float(k + 1), blocks, 0.0), axis=0)
        mass = total[32:33] + total[34:35]
        total = jnp.where(row == 32, mass, jnp.where(row == 34, low_part(mass), total))
        out_ref[k] = total.astype(BF16)


def attend_kernel(sums_ref, qkv_ref, out_ref, token_ref, d_qkv_ref):
    sums = jnp.sum(sums_ref[...].astype(F32), axis=0)
    w_qkv = qkv_ref[...]
    mass = row_to_column(sums[32:33, :] + sums[34:35, :])
    inv = 1.0 / (mass + EPS_MASS)

    def unfold(spread):
        return (spread[:, 0:32] + spread[:, 32:64]) + (spread[:, 64:96] + spread[:, 96:128])

    token = unfold(spread_rows(sums[None, 0:16, :])) * inv
    d_mixed = unfold(spread_rows(sums[None, 16:32, :])).astype(BF16).astype(F32)
    scale = 1.0 / math.sqrt(DH)
    query = dot(token, w_qkv[:, 0:32], precision=HIGHEST)
    keys = dot(token, w_qkv[:, 32:64], precision=HIGHEST)
    values = dot(token, w_qkv[:, 64:96], precision=HIGHEST)
    expo = jnp.exp(dot(query, keys, ((1,), (1,)), HIGHEST) * scale)
    probs = expo / jnp.sum(expo, axis=-1, keepdims=True)
    mixed = dot(probs, values, precision=HIGHEST)
    d_values = dot(probs, d_mixed, ((0,), (0,)), HIGHEST)
    d_probs = dot(d_mixed, values, ((1,), (1,)), HIGHEST)
    d_scores = probs * (d_probs - jnp.sum(probs * d_probs, axis=-1, keepdims=True)) * scale
    d_query = dot(d_scores, keys, precision=HIGHEST)
    d_keys = dot(d_scores, query, ((0,), (0,)), HIGHEST)
    d_qkv = jnp.concatenate([d_query, d_keys, d_values], axis=1)
    token_ref[...] = token
    d_qkv_ref[...] = d_qkv
    d_token = dot(d_qkv, w_qkv, ((1,), (1,)), HIGHEST)
    d_table = d_token * inv
    d_mass = -jnp.sum(d_token * token, axis=1, keepdims=True) * inv

    def pack(values):
        return pack_rows(jnp.concatenate([values] * 4, axis=1))[0]

    tail = column_to_row(d_mass)
    row = iota((8, 128), 0)
    tail = jnp.where(row == 0, tail, jnp.where(row == 2, low_part(tail), 0.0))
    packed = jnp.concatenate([pack(mixed), pack(d_table), tail], axis=0).astype(BF16)
    out_ref[...] = jnp.broadcast_to(packed[None], (OWNERS, 40, 128))


def choose_kernel(blocks_ref, meshes_ref, out_ref):
    numbers = blocks_ref[...].astype(F32)[:, 33:34, :]
    meshes = meshes_ref[...].astype(F32)
    for b in range(2 * HEADS):
        chosen = jnp.zeros((40, 128), F32)
        for k in range(OWNERS):
            chosen = jnp.where(numbers[b] == float(k + 1), meshes[k], chosen)
        out_ref[b] = chosen.astype(BF16)


def back_kernel(
    normed_ref, mid_ref, feat_ref, sw_ref, dout_ref, scaled_ref, weights_ref, g_ref, blocks_ref, temper_ref, tokens_ref,
    mine_ref, other_ref, dmid_ref, dfeat_ref, slice_ref, heat_ref,
):
    tokens = jnp.sum(tokens_ref[...].astype(F32).reshape(2, HEADS, 40, 128), axis=0)
    blocks = blocks_ref[...]
    fold = fold_matrix()
    diagonal = (iota((256, 128), 0) >> 6) == (iota((256, 128), 1) >> 5)
    low_half = iota((1, 128), 1) < 64
    feat = feat_ref[...]
    d_out = dout_ref[...]
    outs, d_mids, d_feats, slabs = [], [], [], []
    temper_grad = jnp.zeros((1, 128), F32)
    lane = iota((1, 128), 1)

    def block_of(packed):
        tiled = dot(spread_rows(packed).astype(BF16), fold)
        return jnp.where(diagonal, tiled, 0.0).astype(BF16)

    for group in range(2):
        lanes = slice(group * 128, (group + 1) * 128)
        wide = slice(group * 256, (group + 1) * 256)
        heads = tokens[4 * group : 4 * group + 4]
        chosen = jnp.concatenate([block_of(heads[:, 0:16]), block_of(heads[:, 16:32])], axis=1)
        d_mass = jnp.concatenate([row_to_column(heads[i, 32:33, :] + heads[i, 34:35, :]) for i in range(4)], axis=0)
        pair = dot(chosen, sw_ref[wide, :], ((0,), (0,)))
        outs.append(pair[:128].astype(BF16))
        d_feats.append(pair[128:].astype(BF16))
        left = jnp.concatenate([d_out[:, lanes], feat[:, lanes]], axis=1)
        d_sw = dot(chosen, left, ((1,), (1,))).astype(BF16).astype(F32)
        d_weights = d_sw + d_mass
        inv_temper = temper_ref[wide, :]
        weights = weights_ref[wide, :]
        d_scaled = weights * (d_weights - head_sums(weights * d_weights))
        products = jnp.sum((d_scaled * scaled_ref[wide, :]).reshape(4, SLICES, ROWS), axis=1)
        totals = jnp.sum(products, axis=1, keepdims=True)
        for i in range(4):
            total = -totals[i : i + 1] * inv_temper[64 * i : 64 * i + 1]
            temper_grad = jnp.where(lane == 4 * group + i, total, temper_grad)
        d_logits = (d_scaled * inv_temper).astype(BF16)
        d_block = dot(mid_ref[lanes, :], d_logits, ((1,), (1,)))
        for i in range(4):
            slabs.append(d_block[i * 32 : (i + 1) * 32, (i // 2) * 128 : (i // 2 + 1) * 128])
        d_mids.append(dot(blocks, d_logits).astype(BF16))
    heat_ref[...] = temper_grad
    slice_ref[...] = jnp.where(
        low_half, (slabs[0] + slabs[2]) + (slabs[4] + slabs[6]), (slabs[1] + slabs[3]) + (slabs[5] + slabs[7])
    )
    d_mid = jnp.concatenate(d_mids, axis=0)
    d_feat = jnp.concatenate(d_feats, axis=0)
    dmid_ref[...] = d_mid
    dfeat_ref[...] = d_feat
    out_grad = dot(jnp.concatenate(outs, axis=0), g_ref[...])
    in_grads = dot(normed_ref[...], jnp.concatenate([d_mid, d_feat], axis=0), ((0,), (1,)))
    halves = []
    for lanes in (slice(0, 128), slice(128, 256)):
        pieces = [out_grad[:, lanes], in_grads[:, :256][:, lanes], in_grads[:, 256:][:, lanes]]
        halves.append(jnp.concatenate([piece.reshape(PEERS, SHARE, 128) for piece in pieces], axis=1))
    first = lax.axis_index("c") == 0
    mine_ref[...] = jnp.where(first, halves[0], halves[1]).astype(BF16)
    other_ref[...] = jnp.where(first, halves[1], halves[0]).astype(BF16)


def norm_kernel(
    dmid_ref, dfeat_ref, wx_ref, wfx_ref, xhat_ref, rstd_ref, gain_ref, g_ref, slice_ref, heat_ref, token_ref, d_qkv_ref,
    feats_ref, small_ref,
):
    d_normed = dot(dmid_ref[...], wx_ref[...], ((0,), (1,))) + dot(dfeat_ref[...], wfx_ref[...], ((0,), (1,)))
    d_normed = d_normed.astype(BF16).astype(F32)
    xhat = xhat_ref[...]
    gain_grad = jnp.sum(d_normed * xhat, axis=0, keepdims=True)
    d_xhat = d_normed * gain_ref[...]
    d_x = rstd_ref[...] * (
        d_xhat
        - jnp.mean(d_xhat, axis=-1, keepdims=True)
        - xhat * jnp.mean(d_xhat * xhat, axis=-1, keepdims=True)
    )
    feats_ref[...] = (g_ref[...].astype(F32) + d_x).astype(BF16)
    qkv_grad = dot(token_ref[...], d_qkv_ref[...], ((0,), (0,)), HIGHEST)
    row = iota((8, 128), 0)
    vectors = jnp.where(row == 0, gain_grad[:, :128], jnp.where(row == 1, gain_grad[:, 128:], 0.0))
    small_ref[0:32, :] = slice_ref[...]
    small_ref[32:64, :] = jnp.concatenate([qkv_grad, jnp.zeros((DH, 32), F32)], axis=1)
    small_ref[64:72, :] = jnp.where(row == 2, heat_ref[...], vectors)
    small_ref[72:, :] = jnp.zeros((WIDTH - 72, 128), F32)


def add_kernel(a_ref, b_ref, small_ref, out_ref):
    total = a_ref[...].astype(F32) + b_ref[...].astype(F32)
    small = small_ref[...].reshape(PEERS, SHARE, 128)
    out_ref[...] = jnp.concatenate([total, small], axis=1).astype(BF16)


def sum_kernel(parts_ref, out_ref):
    total = jnp.sum(parts_ref[...].astype(F32), axis=0).astype(BF16)
    out_ref[...] = jnp.broadcast_to(total[None], out_ref.shape)


def finish_kernel(
    parts_ref,
    gain_hbm, in_x_hbm, in_fx_hbm, slice_hbm, temper_hbm, qkv_hbm, out_hbm,
    gain_ref, in_x_ref, in_fx_ref, slice_ref, temper_ref, qkv_ref, out_ref, sems,
):
    copies = []

    def leave(source, target):
        copies.append(pltpu.make_async_copy(source, target, sems.at[len(copies)]))
        copies[-1].start()

    for at, (ref, hbm) in enumerate(((out_ref, out_hbm), (in_x_ref, in_x_hbm), (in_fx_ref, in_fx_hbm))):
        for half in range(2):
            piece = parts_ref[half * PEERS : (half + 1) * PEERS].astype(F32)[:, at * SHARE : (at + 1) * SHARE]
            ref[:, half * 128 : (half + 1) * 128] = piece.reshape(WIDTH, 128)
        leave(ref, hbm)
    small = parts_ref[:PEERS].astype(F32)[:, 3 * SHARE :] + parts_ref[PEERS:].astype(F32)[:, 3 * SHARE :]
    small = small.reshape(WIDTH, 128)
    slices = small[0:32]
    slice_ref[...] = slices[:, :64] + slices[:, 64:]
    leave(slice_ref, slice_hbm)
    qkv_ref[...] = small[32:64, :96]
    leave(qkv_ref, qkv_hbm)
    gain_ref[:, :128] = small[64:65]
    gain_ref[:, 128:] = small[65:66]
    leave(gain_ref, gain_hbm)
    temper_ref[...] = small[66:67, :8]
    leave(temper_ref, temper_hbm)
    for copy in copies:
        copy.wait()


def call(kernel, name, inputs, outputs, scalars=0, far_in=False, far_out=False, scratch=(), cost=None):
    single = not isinstance(outputs, (list, tuple))
    in_spec = pl.BlockSpec(memory_space=pltpu.HBM if far_in else pltpu.VMEM)
    out_spec = pl.BlockSpec(memory_space=pltpu.HBM if far_out else pltpu.VMEM)
    return pl.pallas_call(
        kernel,
        name=name,
        out_shape=outputs,
        in_specs=[pl.BlockSpec(memory_space=pltpu.SMEM)] * scalars + [in_spec] * (len(inputs) - scalars),
        out_specs=out_spec if single else [out_spec] * len(outputs),
        scratch_shapes=scratch,
        compiler_params=pltpu.CompilerParams(vmem_limit_bytes=48 * 1024 * 1024),
        cost_estimate=cost,
    )(*inputs)


def shape(dims, dtype=BF16):
    return jax.ShapeDtypeStruct(dims, dtype)


def shards(
    node_feats, cotangent, mesh_of_block, block_rows, ln_gain, w_in_x, w_in_fx, w_slice, temper, w_qkv, w_out
):
    x = node_feats.reshape(ROWS, WIDTH)
    cot = cotangent.reshape(ROWS, WIDTH)
    gain = ln_gain.reshape(1, WIDTH)
    wide = shape((ROWS, WIDTH))
    packets = shape((2 * HEADS, 40, 128))
    owned = shape((OWNERS, 40, 128))
    tall = shape((2 * WIDTH, ROWS), F32)
    flat = shape((WIDTH, ROWS))
    inputs = (x, gain, w_in_x, w_in_fx, w_slice, temper.reshape(1, HEADS), cot, w_out)
    far = [pltpu.with_memory_space_constraint(a, pltpu.HBM) for a in inputs]
    scratch = [pltpu.VMEM(a.shape, a.dtype) for a in (x, w_slice, inputs[5], cot, w_out)]
    scratch.append(pltpu.SemaphoreType.DMA((len(far),)))
    send, normed, mid, feat, sw, d_out, scaled, weights, xhat, rstd, gains, wx, wfx, g, diagonal, heat = call(
        front_kernel,
        "front",
        (block_rows, mesh_of_block, *far),
        [
            packets, wide, flat, wide, shape((2 * WIDTH, ROWS)), wide,
            tall, tall, shape((ROWS, WIDTH), F32), shape((ROWS, 1), F32),
            shape((1, WIDTH), F32), shape((WIDTH, WIDTH)), shape((WIDTH, WIDTH)), wide,
            shape((128, 256)), shape((2 * WIDTH, 1), F32),
        ],
        scalars=2,
        far_in=True,
        scratch=scratch,
    )
    blocks = lax.all_to_all(send, ("zl", "y", "c"), 0, 0)
    dense = call(dense_kernel, "dense", (blocks,), owned)
    sums = lax.all_to_all(dense, ("zb", "zc", "za"), 0, 0)
    answer, token, d_qkv = call(
        attend_kernel,
        "attend",
        (sums, w_qkv),
        [owned, shape((SLICES, DH), F32), shape((SLICES, 3 * DH), F32)],
    )
    meshes = lax.all_to_all(answer, ("zb", "zc", "za"), 0, 0)
    chosen = call(choose_kernel, "choose", (blocks, meshes), packets)
    tokens = lax.all_to_all(chosen, ("zl", "y", "c"), 0, 0)
    share = shape((PEERS, 4 * SHARE, 128))
    big = shape((PEERS, 3 * SHARE, 128))
    mine, other, d_mid, d_feat, slice_grad, temper_grad = call(
        back_kernel,
        "back",
        (normed, mid, feat, sw, d_out, scaled, weights, g, diagonal, heat, tokens),
        [big, big, flat, flat, shape((DH, 128), F32), shape((1, 128), F32)],
    )
    other = lax.ppermute(other, "c", [(0, 1), (1, 0)])
    feats_grad, small = call(
        norm_kernel,
        "norm",
        (d_mid, d_feat, wx, wfx, xhat, rstd, gains, g, slice_grad, temper_grad, token, d_qkv),
        [wide, shape((WIDTH, 128), F32)],
        cost=pl.CostEstimate(flops=4 * ROWS * WIDTH * WIDTH, bytes_accessed=4 * 1024 * 1024, transcendentals=0),
    )
    across = ("y", "zl", "x")
    parts = call(add_kernel, "add_pair", (mine, other, small), share)
    parts = lax.all_to_all(parts, across, 0, 0)
    parts = call(sum_kernel, "sum_peers", (parts,), shape((OWNERS, 4 * SHARE, 128)))
    parts = lax.all_to_all(parts, ("zb", "zc", "za"), 0, 0)
    parts = call(sum_kernel, "sum_z", (parts,), share)
    parts = lax.all_to_all(parts, across, 0, 0)
    parts = lax.all_gather(parts, "c", axis=0, tiled=True)
    square = shape((WIDTH, WIDTH), F32)
    results = [
        shape((1, WIDTH), F32), square, square, shape((DH, SLICES), F32),
        shape((1, HEADS), F32), shape((DH, 3 * DH), F32), square,
    ]
    gain_grad, in_x_grad, in_fx_grad, slice_grad, temper_grad, qkv_grad, out_grad = call(
        finish_kernel,
        "finish",
        (parts,),
        results,
        far_out=True,
        scratch=[pltpu.VMEM(r.shape, r.dtype) for r in results] + [pltpu.SemaphoreType.DMA((len(results),))],
    )
    return (
        feats_grad.reshape(1, 1, ROWS, WIDTH),
        gain_grad.reshape(WIDTH),
        in_x_grad,
        in_fx_grad,
        slice_grad,
        temper_grad.reshape(HEADS),
        qkv_grad,
        out_grad,
    )


def solution(mesh):
    groups = mesh.shape["dp"]
    devices = mesh.devices.reshape(4, 2, 2, 2, 2, 2, groups)
    grid = Mesh(devices, ("y", "za", "zb", "zc", "zl", "c", "x"))
    node = ("y", "za", "zb", "zc", "zl", "c")
    blocks = P("x", node, None, None)
    scalars = P("x", node)
    return jax.shard_map(
        shards,
        mesh=grid,
        in_specs=(blocks, blocks, scalars, scalars) + (P(),) * 7,
        out_specs=(blocks,) + (P(),) * 7,
        check_vma=False,
    )
```

```python
import math

import jax
import jax.numpy as jnp
from jax import lax
from jax.experimental import pallas as pl
from jax.experimental.pallas import tpu as pltpu
from jax.sharding import Mesh
from jax.sharding import PartitionSpec as P

EPS_NORM = 1e-05
EPS_MASS = 1e-05
HEADS = 8
DH = 32
SLICES = 64
WIDTH = 256
ROWS = 512
OWNERS = 8
PEERS = 32
SHARE = 8
F32 = jnp.float32
BF16 = jnp.bfloat16
HIGHEST = lax.Precision.HIGHEST


def iota(shape, dim):
    return lax.broadcasted_iota(jnp.int32, shape, dim)


def dot(a, b, dims=((1,), (0,)), precision=None):
    return lax.dot_general(a, b, (dims, ((), ())), precision=precision, preferred_element_type=F32)


def four_blocks(w_slice):
    two = jnp.concatenate([w_slice, w_slice], axis=1)
    four = jnp.concatenate([two, two], axis=1)
    tall = jnp.concatenate([four] * 4, axis=0)
    same = (iota((128, 256), 0) >> 5) == (iota((128, 256), 1) >> 6)
    return jnp.where(same, tall, 0.0).astype(BF16)


def fold_matrix():
    return ((iota((128, 128), 0) & 31) == (iota((128, 128), 1) & 31)).astype(F32).astype(BF16)


def quarter_mask(rows):
    return ((iota((rows, 128), 0) & 63) >> 4) == (iota((rows, 128), 1) >> 5)


def pack_rows(tiled):
    rows = tiled.shape[0]
    kept = jnp.where(quarter_mask(rows), tiled, 0.0)
    return jnp.sum(kept.reshape(rows // 64, 4, 16, 128), axis=1)


def spread_rows(packed):
    heads = packed.shape[0]
    tall = jnp.broadcast_to(packed[:, None], (heads, 4, 16, 128)).reshape(heads * 64, 128)
    return jnp.where(quarter_mask(heads * 64), tall, 0.0)


def temper_column(temper, group):
    head = iota((256, 1), 0) >> 6
    column = jnp.zeros((256, 1), F32)
    for i in range(4):
        column = jnp.where(head == i, temper[:, 4 * group + i : 4 * group + i + 1], column)
    return column


def head_sums(values):
    rows, nodes = values.shape
    sums = jnp.sum(values.reshape(rows // 64, 64, nodes), axis=1, keepdims=True)
    return jnp.broadcast_to(sums, (rows // 64, 64, nodes)).reshape(rows, nodes)


def eye_mask():
    return iota((SLICES, 128), 0) == iota((SLICES, 128), 1)


def column_to_row(column):
    return jnp.sum(jnp.where(eye_mask(), column, 0.0), axis=0, keepdims=True)


def row_to_column(row):
    return jnp.sum(jnp.where(eye_mask(), row, 0.0), axis=1, keepdims=True)


def low_part(values):
    return values - values.astype(BF16).astype(F32)


def normalise(x):
    xf = x.astype(F32)
    mean = jnp.mean(xf, axis=-1, keepdims=True)
    centered = xf - mean
    var = jnp.mean(centered * centered, axis=-1, keepdims=True)
    rstd = lax.rsqrt(var + EPS_NORM)
    return centered * rstd, rstd


def front_kernel(
    rows_ref, mesh_ref, x_hbm, gain_hbm, wx_hbm, wfx_hbm, slice_hbm, temper_hbm, cot_hbm, wout_hbm,
    send_ref, normed_ref, mid_ref, feat_ref, sw_ref, dout_ref, scaled_ref, weights_ref, xhat_ref, rstd_ref,
    gain_ref, wx_ref, wfx_ref, g_ref, blocks_ref, temper_ref,
    x_ref, slice_ref, heat_ref, cot_ref, wout_ref, sems,
):
    sources = (x_hbm, gain_hbm, wx_hbm, wfx_hbm, slice_hbm, temper_hbm, cot_hbm, wout_hbm)
    targets = (x_ref, gain_ref, wx_ref, wfx_ref, slice_ref, heat_ref, cot_ref, wout_ref)
    copies = [pltpu.make_async_copy(a, b, sems.at[i]) for i, (a, b) in enumerate(zip(sources, targets))]
    for copy in copies:
        copy.start()
    copies[0].wait()
    xhat, rstd = normalise(x_ref[...])
    xhat_ref[...] = xhat
    rstd_ref[...] = rstd
    for copy in copies[1:]:
        copy.wait()
    normed = (xhat * gain_ref[...]).astype(BF16)
    normed_ref[...] = normed
    mid = dot(wx_ref[...], normed, ((0,), (1,))).astype(BF16)
    feat = dot(normed, wfx_ref[...]).astype(BF16)
    mid_ref[...] = mid
    feat_ref[...] = feat
    blocks = four_blocks(slice_ref[...])
    blocks_ref[...] = blocks
    heat = heat_ref[...]
    g_b = jnp.where(iota((ROWS, 1), 0) < rows_ref[0, 0], cot_ref[...].astype(F32), 0.0).astype(BF16)
    g_ref[...] = g_b
    d_out = dot(g_b, wout_ref[...], ((1,), (1,))).astype(BF16)
    dout_ref[...] = d_out
    fold = fold_matrix()
    diagonal = (iota((256, 256), 0) >> 6) == ((iota((256, 256), 1) & 127) >> 5)
    valid = (iota((1, ROWS), 1) < rows_ref[0, 0]).astype(F32)
    tables, grads, masses = [], [], []
    for group in range(2):
        lanes = slice(group * 128, (group + 1) * 128)
        wide = slice(group * 256, (group + 1) * 256)
        inv_temper = 1.0 / temper_column(heat, group)
        temper_ref[wide, :] = inv_temper
        scaled = dot(blocks, mid[lanes], ((0,), (0,))) * inv_temper
        expo = jnp.exp(scaled)
        weights = expo / head_sums(expo) * valid
        sw = weights.astype(BF16)
        scaled_ref[wide, :] = scaled
        weights_ref[wide, :] = weights
        sw_ref[wide, :] = sw
        both = jnp.concatenate([feat[:, lanes], d_out[:, lanes]], axis=1)
        full = jnp.where(diagonal, dot(sw, both), 0.0).astype(BF16)
        tables.append(pack_rows(dot(full[:, :128], fold)))
        grads.append(pack_rows(dot(full[:, 128:], fold)))
        mass = jnp.sum(weights, axis=1, keepdims=True)
        masses += [column_to_row(mass[64 * i : 64 * i + 64]) for i in range(4)]
    row = iota((8, 128), 0)
    mesh = mesh_ref[0, 0]
    number = jnp.where(row == 1, ((mesh >> 1) + 1).astype(F32), 0.0)
    tails = [jnp.where(row == 0, mass, jnp.where(row == 2, low_part(mass), number))[None] for mass in masses]
    packed = [jnp.concatenate(tables, axis=0), jnp.concatenate(grads, axis=0), jnp.concatenate(tails, axis=0)]
    packed = jnp.concatenate(packed, axis=1)
    odd = (mesh & 1).astype(F32)
    send_ref[...] = jnp.concatenate([packed * (1.0 - odd), packed * odd], axis=0).astype(BF16)


def dense_kernel(blocks_ref, out_ref):
    blocks = blocks_ref[...].astype(F32)
    numbers = blocks[:, 33:34, :]
    row = iota((40, 128), 0)
    for k in range(OWNERS):
        total = jnp.sum(jnp.where(numbers == float(k + 1), blocks, 0.0), axis=0)
        mass = total[32:33] + total[34:35]
        total = jnp.where(row == 32, mass, jnp.where(row == 34, low_part(mass), total))
        out_ref[k] = total.astype(BF16)


def attend_kernel(sums_ref, qkv_ref, out_ref, token_ref, d_qkv_ref):
    sums = jnp.sum(sums_ref[...].astype(F32), axis=0)
    w_qkv = qkv_ref[...]
    mass = row_to_column(sums[32:33, :] + sums[34:35, :])
    inv = 1.0 / (mass + EPS_MASS)

    def unfold(spread):
        return (spread[:, 0:32] + spread[:, 32:64]) + (spread[:, 64:96] + spread[:, 96:128])

    token = unfold(spread_rows(sums[None, 0:16, :])) * inv
    d_mixed = unfold(spread_rows(sums[None, 16:32, :])).astype(BF16).astype(F32)
    scale = 1.0 / math.sqrt(DH)
    query = dot(token, w_qkv[:, 0:32], precision=HIGHEST)
    keys = dot(token, w_qkv[:, 32:64], precision=HIGHEST)
    values = dot(token, w_qkv[:, 64:96], precision=HIGHEST)
    expo = jnp.exp(dot(query, keys, ((1,), (1,)), HIGHEST) * scale)
    probs = expo / jnp.sum(expo, axis=-1, keepdims=True)
    mixed = dot(probs, values, precision=HIGHEST)
    d_values = dot(probs, d_mixed, ((0,), (0,)), HIGHEST)
    d_probs = dot(d_mixed, values, ((1,), (1,)), HIGHEST)
    d_scores = probs * (d_probs - jnp.sum(probs * d_probs, axis=-1, keepdims=True)) * scale
    d_query = dot(d_scores, keys, precision=HIGHEST)
    d_keys = dot(d_scores, query, ((0,), (0,)), HIGHEST)
    d_qkv = jnp.concatenate([d_query, d_keys, d_values], axis=1)
    token_ref[...] = token
    d_qkv_ref[...] = d_qkv
    d_token = dot(d_qkv, w_qkv, ((1,), (1,)), HIGHEST)
    d_table = d_token * inv
    d_mass = -jnp.sum(d_token * token, axis=1, keepdims=True) * inv

    def pack(values):
        return pack_rows(jnp.concatenate([values] * 4, axis=1))[0]

    tail = column_to_row(d_mass)
    row = iota((8, 128), 0)
    tail = jnp.where(row == 0, tail, jnp.where(row == 2, low_part(tail), 0.0))
    packed = jnp.concatenate([pack(mixed), pack(d_table), tail], axis=0).astype(BF16)
    out_ref[...] = jnp.broadcast_to(packed[None], (OWNERS, 40, 128))


def choose_kernel(blocks_ref, meshes_ref, out_ref):
    numbers = blocks_ref[...].astype(F32)[:, 33:34, :]
    meshes = meshes_ref[...].astype(F32)
    for b in range(2 * HEADS):
        chosen = jnp.zeros((40, 128), F32)
        for k in range(OWNERS):
            chosen = jnp.where(numbers[b] == float(k + 1), meshes[k], chosen)
        out_ref[b] = chosen.astype(BF16)


def back_kernel(
    normed_ref, mid_ref, feat_ref, sw_ref, dout_ref, scaled_ref, weights_ref, g_ref, blocks_ref, temper_ref, tokens_ref,
    mine_ref, other_ref, dmid_ref, dfeat_ref, slice_ref, heat_ref,
):
    tokens = jnp.sum(tokens_ref[...].astype(F32).reshape(2, HEADS, 40, 128), axis=0)
    blocks = blocks_ref[...]
    fold = fold_matrix()
    diagonal = (iota((256, 128), 0) >> 6) == (iota((256, 128), 1) >> 5)
    low_half = iota((1, 128), 1) < 64
    feat = feat_ref[...]
    d_out = dout_ref[...]
    outs, d_mids, d_feats, slabs = [], [], [], []
    temper_grad = jnp.zeros((1, 128), F32)
    lane = iota((1, 128), 1)

    def block_of(packed):
        tiled = dot(spread_rows(packed).astype(BF16), fold)
        return jnp.where(diagonal, tiled, 0.0).astype(BF16)

    for group in range(2):
        lanes = slice(group * 128, (group + 1) * 128)
        wide = slice(group * 256, (group + 1) * 256)
        heads = tokens[4 * group : 4 * group + 4]
        chosen = jnp.concatenate([block_of(heads[:, 0:16]), block_of(heads[:, 16:32])], axis=1)
        d_mass = jnp.concatenate([row_to_column(heads[i, 32:33, :] + heads[i, 34:35, :]) for i in range(4)], axis=0)
        pair = dot(chosen, sw_ref[wide, :], ((0,), (0,)))
        outs.append(pair[:128].astype(BF16))
        d_feats.append(pair[128:].astype(BF16))
        left = jnp.concatenate([d_out[:, lanes], feat[:, lanes]], axis=1)
        d_sw = dot(chosen, left, ((1,), (1,))).astype(BF16).astype(F32)
        d_weights = d_sw + d_mass
        inv_temper = temper_ref[wide, :]
        weights = weights_ref[wide, :]
        d_scaled = weights * (d_weights - head_sums(weights * d_weights))
        products = jnp.sum((d_scaled * scaled_ref[wide, :]).reshape(4, SLICES, ROWS), axis=1)
        totals = jnp.sum(products, axis=1, keepdims=True)
        for i in range(4):
            total = -totals[i : i + 1] * inv_temper[64 * i : 64 * i + 1]
            temper_grad = jnp.where(lane == 4 * group + i, total, temper_grad)
        d_logits = (d_scaled * inv_temper).astype(BF16)
        d_block = dot(mid_ref[lanes, :], d_logits, ((1,), (1,)))
        for i in range(4):
            slabs.append(d_block[i * 32 : (i + 1) * 32, (i // 2) * 128 : (i // 2 + 1) * 128])
        d_mids.append(dot(blocks, d_logits).astype(BF16))
    heat_ref[...] = temper_grad
    slice_ref[...] = jnp.where(
        low_half, (slabs[0] + slabs[2]) + (slabs[4] + slabs[6]), (slabs[1] + slabs[3]) + (slabs[5] + slabs[7])
    )
    d_mid = jnp.concatenate(d_mids, axis=0)
    d_feat = jnp.concatenate(d_feats, axis=0)
    dmid_ref[...] = d_mid
    dfeat_ref[...] = d_feat
    out_grad = dot(jnp.concatenate(outs, axis=0), g_ref[...])
    in_grads = dot(normed_ref[...], jnp.concatenate([d_mid, d_feat], axis=0), ((0,), (1,)))
    halves = []
    for lanes in (slice(0, 128), slice(128, 256)):
        pieces = [out_grad[:, lanes], in_grads[:, :256][:, lanes], in_grads[:, 256:][:, lanes]]
        halves.append(jnp.concatenate([piece.reshape(PEERS, SHARE, 128) for piece in pieces], axis=1))
    first = lax.axis_index("c") == 0
    mine_ref[...] = jnp.where(first, halves[0], halves[1]).astype(BF16)
    other_ref[...] = jnp.where(first, halves[1], halves[0]).astype(BF16)


def norm_kernel(
    dmid_ref, dfeat_ref, wx_ref, wfx_ref, xhat_ref, rstd_ref, gain_ref, g_ref, slice_ref, heat_ref, token_ref, d_qkv_ref,
    feats_ref, small_ref,
):
    d_normed = dot(dmid_ref[...], wx_ref[...], ((0,), (1,))) + dot(dfeat_ref[...], wfx_ref[...], ((0,), (1,)))
    d_normed = d_normed.astype(BF16).astype(F32)
    xhat = xhat_ref[...]
    gain_grad = jnp.sum(d_normed * xhat, axis=0, keepdims=True)
    d_xhat = d_normed * gain_ref[...]
    d_x = rstd_ref[...] * (
        d_xhat
        - jnp.mean(d_xhat, axis=-1, keepdims=True)
        - xhat * jnp.mean(d_xhat * xhat, axis=-1, keepdims=True)
    )
    feats_ref[...] = (g_ref[...].astype(F32) + d_x).astype(BF16)
    qkv_grad = dot(token_ref[...], d_qkv_ref[...], ((0,), (0,)), HIGHEST)
    row = iota((8, 128), 0)
    vectors = jnp.where(row == 0, gain_grad[:, :128], jnp.where(row == 1, gain_grad[:, 128:], 0.0))
    small_ref[0:32, :] = slice_ref[...]
    small_ref[32:64, :] = jnp.concatenate([qkv_grad, jnp.zeros((DH, 32), F32)], axis=1)
    small_ref[64:72, :] = jnp.where(row == 2, heat_ref[...], vectors)
    small_ref[72:, :] = jnp.zeros((WIDTH - 72, 128), F32)


def add_kernel(a_ref, b_ref, small_ref, out_ref):
    total = a_ref[...].astype(F32) + b_ref[...].astype(F32)
    small = small_ref[...].reshape(PEERS, SHARE, 128)
    out_ref[...] = jnp.concatenate([total, small], axis=1).astype(BF16)


def sum_kernel(parts_ref, out_ref):
    total = jnp.sum(parts_ref[...].astype(F32), axis=0).astype(BF16)
    out_ref[...] = jnp.broadcast_to(total[None], out_ref.shape)


def finish_kernel(
    parts_ref,
    gain_hbm, in_x_hbm, in_fx_hbm, slice_hbm, temper_hbm, qkv_hbm, out_hbm,
    gain_ref, in_x_ref, in_fx_ref, slice_ref, temper_ref, qkv_ref, out_ref, sems,
):
    copies = []

    def leave(source, target):
        copies.append(pltpu.make_async_copy(source, target, sems.at[len(copies)]))
        copies[-1].start()

    for at, (ref, hbm) in enumerate(((out_ref, out_hbm), (in_x_ref, in_x_hbm), (in_fx_ref, in_fx_hbm))):
        for half in range(2):
            piece = parts_ref[half * PEERS : (half + 1) * PEERS].astype(F32)[:, at * SHARE : (at + 1) * SHARE]
            ref[:, half * 128 : (half + 1) * 128] = piece.reshape(WIDTH, 128)
        leave(ref, hbm)
    small = parts_ref[:PEERS].astype(F32)[:, 3 * SHARE :] + parts_ref[PEERS:].astype(F32)[:, 3 * SHARE :]
    small = small.reshape(WIDTH, 128)
    slices = small[0:32]
    slice_ref[...] = slices[:, :64] + slices[:, 64:]
    leave(slice_ref, slice_hbm)
    qkv_ref[...] = small[32:64, :96]
    leave(qkv_ref, qkv_hbm)
    gain_ref[:, :128] = small[64:65]
    gain_ref[:, 128:] = small[65:66]
    leave(gain_ref, gain_hbm)
    temper_ref[...] = small[66:67, :8]
    leave(temper_ref, temper_hbm)
    for copy in copies:
        copy.wait()


def call(kernel, name, inputs, outputs, scalars=0, far_in=False, far_out=False, scratch=(), cost=None):
    single = not isinstance(outputs, (list, tuple))
    in_spec = pl.BlockSpec(memory_space=pltpu.HBM if far_in else pltpu.VMEM)
    out_spec = pl.BlockSpec(memory_space=pltpu.HBM if far_out else pltpu.VMEM)
    return pl.pallas_call(
        kernel,
        name=name,
        out_shape=outputs,
        in_specs=[pl.BlockSpec(memory_space=pltpu.SMEM)] * scalars + [in_spec] * (len(inputs) - scalars),
        out_specs=out_spec if single else [out_spec] * len(outputs),
        scratch_shapes=scratch,
        compiler_params=pltpu.CompilerParams(vmem_limit_bytes=48 * 1024 * 1024),
        cost_estimate=cost,
    )(*inputs)


def shape(dims, dtype=BF16):
    return jax.ShapeDtypeStruct(dims, dtype)


def shards(
    node_feats, cotangent, mesh_of_block, block_rows, ln_gain, w_in_x, w_in_fx, w_slice, temper, w_qkv, w_out
):
    x = node_feats.reshape(ROWS, WIDTH)
    cot = cotangent.reshape(ROWS, WIDTH)
    gain = ln_gain.reshape(1, WIDTH)
    wide = shape((ROWS, WIDTH))
    packets = shape((2 * HEADS, 40, 128))
    owned = shape((OWNERS, 40, 128))
    tall = shape((2 * WIDTH, ROWS), F32)
    flat = shape((WIDTH, ROWS))
    inputs = (x, gain, w_in_x, w_in_fx, w_slice, temper.reshape(1, HEADS), cot, w_out)
    far = [pltpu.with_memory_space_constraint(a, pltpu.HBM) for a in inputs]
    scratch = [pltpu.VMEM(a.shape, a.dtype) for a in (x, w_slice, inputs[5], cot, w_out)]
    scratch.append(pltpu.SemaphoreType.DMA((len(far),)))
    send, normed, mid, feat, sw, d_out, scaled, weights, xhat, rstd, gains, wx, wfx, g, diagonal, heat = call(
        front_kernel,
        "front",
        (block_rows, mesh_of_block, *far),
        [
            packets, wide, flat, wide, shape((2 * WIDTH, ROWS)), wide,
            tall, tall, shape((ROWS, WIDTH), F32), shape((ROWS, 1), F32),
            shape((1, WIDTH), F32), shape((WIDTH, WIDTH)), shape((WIDTH, WIDTH)), wide,
            shape((128, 256)), shape((2 * WIDTH, 1), F32),
        ],
        scalars=2,
        far_in=True,
        scratch=scratch,
    )
    blocks = lax.all_to_all(send, ("zl", "y", "c"), 0, 0)
    dense = call(dense_kernel, "dense", (blocks,), owned)
    sums = lax.all_to_all(dense, ("zb", "zc", "za"), 0, 0)
    answer, token, d_qkv = call(
        attend_kernel,
        "attend",
        (sums, w_qkv),
        [owned, shape((SLICES, DH), F32), shape((SLICES, 3 * DH), F32)],
    )
    meshes = lax.all_to_all(answer, ("zb", "zc", "za"), 0, 0)
    chosen = call(choose_kernel, "choose", (blocks, meshes), packets)
    tokens = lax.all_to_all(chosen, ("zl", "y", "c"), 0, 0)
    share = shape((PEERS, 4 * SHARE, 128))
    big = shape((PEERS, 3 * SHARE, 128))
    mine, other, d_mid, d_feat, slice_grad, temper_grad = call(
        back_kernel,
        "back",
        (normed, mid, feat, sw, d_out, scaled, weights, g, diagonal, heat, tokens),
        [big, big, flat, flat, shape((DH, 128), F32), shape((1, 128), F32)],
    )
    other = lax.ppermute(other, "c", [(0, 1), (1, 0)])
    feats_grad, small = call(
        norm_kernel,
        "norm",
        (d_mid, d_feat, wx, wfx, xhat, rstd, gains, g, slice_grad, temper_grad, token, d_qkv),
        [wide, shape((WIDTH, 128), F32)],
        cost=pl.CostEstimate(flops=4 * ROWS * WIDTH * WIDTH, bytes_accessed=4 * 1024 * 1024, transcendentals=0),
    )
    across = ("y", "zl", "x")
    parts = call(add_kernel, "add_pair", (mine, other, small), share)
    parts = lax.all_to_all(parts, across, 0, 0)
    parts = call(sum_kernel, "sum_peers", (parts,), shape((OWNERS, 4 * SHARE, 128)))
    parts = lax.all_to_all(parts, ("zb", "zc", "za"), 0, 0)
    parts = call(sum_kernel, "sum_z", (parts,), share)
    parts = lax.all_to_all(parts, across, 0, 0)
    parts = lax.all_gather(parts, "c", axis=0, tiled=True)
    square = shape((WIDTH, WIDTH), F32)
    results = [
        shape((1, WIDTH), F32), square, square, shape((DH, SLICES), F32),
        shape((1, HEADS), F32), shape((DH, 3 * DH), F32), square,
    ]
    gain_grad, in_x_grad, in_fx_grad, slice_grad, temper_grad, qkv_grad, out_grad = call(
        finish_kernel,
        "finish",
        (parts,),
        results,
        far_out=True,
        scratch=[pltpu.VMEM(r.shape, r.dtype) for r in results] + [pltpu.SemaphoreType.DMA((len(results),))],
    )
    return (
        feats_grad.reshape(1, 1, ROWS, WIDTH),
        gain_grad.reshape(WIDTH),
        in_x_grad,
        in_fx_grad,
        slice_grad,
        temper_grad.reshape(HEADS),
        qkv_grad,
        out_grad,
    )


def solution(mesh):
    groups = mesh.shape["dp"]
    devices = mesh.devices.reshape(4, 2, 2, 2, 2, 2, groups)
    grid = Mesh(devices, ("y", "za", "zb", "zc", "zl", "c", "x"))
    node = ("y", "za", "zb", "zc", "zl", "c")
    blocks = P("x", node, None, None)
    scalars = P("x", node)
    return jax.shard_map(
        shards,
        mesh=grid,
        in_specs=(blocks, blocks, scalars, scalars) + (P(),) * 7,
        out_specs=(blocks,) + (P(),) * 7,
        check_vma=False,
    )
```

```python
import math

import jax
import jax.numpy as jnp
from jax import lax
from jax.experimental import pallas as pl
from jax.experimental.pallas import tpu as pltpu
from jax.sharding import Mesh
from jax.sharding import PartitionSpec as P

EPS_NORM = 1e-05
EPS_MASS = 1e-05
HEADS = 8
DH = 32
SLICES = 64
WIDTH = 256
ROWS = 512
OWNERS = 8
PEERS = 32
SHARE = 8
F32 = jnp.float32
BF16 = jnp.bfloat16
HIGHEST = lax.Precision.HIGHEST


def iota(shape, dim):
    return lax.broadcasted_iota(jnp.int32, shape, dim)


def dot(a, b, dims=((1,), (0,)), precision=None):
    return lax.dot_general(a, b, (dims, ((), ())), precision=precision, preferred_element_type=F32)


def four_blocks(w_slice):
    two = jnp.concatenate([w_slice, w_slice], axis=1)
    four = jnp.concatenate([two, two], axis=1)
    tall = jnp.concatenate([four] * 4, axis=0)
    same = (iota((128, 256), 0) >> 5) == (iota((128, 256), 1) >> 6)
    return jnp.where(same, tall, 0.0).astype(BF16)


def fold_matrix():
    return ((iota((128, 128), 0) & 31) == (iota((128, 128), 1) & 31)).astype(F32).astype(BF16)


def quarter_mask(rows):
    return ((iota((rows, 128), 0) & 63) >> 4) == (iota((rows, 128), 1) >> 5)


def pack_rows(tiled):
    rows = tiled.shape[0]
    kept = jnp.where(quarter_mask(rows), tiled, 0.0)
    return jnp.sum(kept.reshape(rows // 64, 4, 16, 128), axis=1)


def spread_rows(packed):
    heads = packed.shape[0]
    tall = jnp.broadcast_to(packed[:, None], (heads, 4, 16, 128)).reshape(heads * 64, 128)
    return jnp.where(quarter_mask(heads * 64), tall, 0.0)


def temper_column(temper, group):
    head = iota((256, 1), 0) >> 6
    column = jnp.zeros((256, 1), F32)
    for i in range(4):
        column = jnp.where(head == i, temper[:, 4 * group + i : 4 * group + i + 1], column)
    return column


def head_sums(values):
    rows, nodes = values.shape
    sums = jnp.sum(values.reshape(rows // 64, 64, nodes), axis=1, keepdims=True)
    return jnp.broadcast_to(sums, (rows // 64, 64, nodes)).reshape(rows, nodes)


def eye_mask():
    return iota((SLICES, 128), 0) == iota((SLICES, 128), 1)


def column_to_row(column):
    return jnp.sum(jnp.where(eye_mask(), column, 0.0), axis=0, keepdims=True)


def row_to_column(row):
    return jnp.sum(jnp.where(eye_mask(), row, 0.0), axis=1, keepdims=True)


def low_part(values):
    return values - values.astype(BF16).astype(F32)


def normalise(x):
    xf = x.astype(F32)
    mean = jnp.mean(xf, axis=-1, keepdims=True)
    centered = xf - mean
    var = jnp.mean(centered * centered, axis=-1, keepdims=True)
    rstd = lax.rsqrt(var + EPS_NORM)
    return centered * rstd, rstd


def front_kernel(
    rows_ref, mesh_ref, x_hbm, gain_hbm, wx_hbm, wfx_hbm, slice_hbm, temper_hbm, cot_hbm, wout_hbm,
    send_ref, normed_ref, mid_ref, feat_ref, sw_ref, dout_ref, scaled_ref, weights_ref, xhat_ref, rstd_ref,
    gain_ref, wx_ref, wfx_ref, g_ref, blocks_ref, temper_ref,
    x_ref, slice_ref, heat_ref, cot_ref, wout_ref, sems,
):
    sources = (x_hbm, gain_hbm, wx_hbm, wfx_hbm, slice_hbm, temper_hbm, cot_hbm, wout_hbm)
    targets = (x_ref, gain_ref, wx_ref, wfx_ref, slice_ref, heat_ref, cot_ref, wout_ref)
    copies = [pltpu.make_async_copy(a, b, sems.at[i]) for i, (a, b) in enumerate(zip(sources, targets))]
    for copy in copies:
        copy.start()
    copies[0].wait()
    xhat, rstd = normalise(x_ref[...])
    xhat_ref[...] = xhat
    rstd_ref[...] = rstd
    for copy in copies[1:]:
        copy.wait()
    normed = (xhat * gain_ref[...]).astype(BF16)
    normed_ref[...] = normed
    mid = dot(wx_ref[...], normed, ((0,), (1,))).astype(BF16)
    feat = dot(normed, wfx_ref[...]).astype(BF16)
    mid_ref[...] = mid
    feat_ref[...] = feat
    blocks = four_blocks(slice_ref[...])
    blocks_ref[...] = blocks
    heat = heat_ref[...]
    g_b = jnp.where(iota((ROWS, 1), 0) < rows_ref[0, 0], cot_ref[...].astype(F32), 0.0).astype(BF16)
    g_ref[...] = g_b
    d_out = dot(g_b, wout_ref[...], ((1,), (1,))).astype(BF16)
    dout_ref[...] = d_out
    fold = fold_matrix()
    diagonal = (iota((256, 256), 0) >> 6) == ((iota((256, 256), 1) & 127) >> 5)
    valid = (iota((1, ROWS), 1) < rows_ref[0, 0]).astype(F32)
    tables, grads, masses = [], [], []
    for group in range(2):
        lanes = slice(group * 128, (group + 1) * 128)
        wide = slice(group * 256, (group + 1) * 256)
        inv_temper = 1.0 / temper_column(heat, group)
        temper_ref[wide, :] = inv_temper
        scaled = dot(blocks, mid[lanes], ((0,), (0,))) * inv_temper
        expo = jnp.exp(scaled)
        weights = expo / head_sums(expo) * valid
        sw = weights.astype(BF16)
        scaled_ref[wide, :] = scaled
        weights_ref[wide, :] = weights
        sw_ref[wide, :] = sw
        both = jnp.concatenate([feat[:, lanes], d_out[:, lanes]], axis=1)
        full = jnp.where(diagonal, dot(sw, both), 0.0).astype(BF16)
        tables.append(pack_rows(dot(full[:, :128], fold)))
        grads.append(pack_rows(dot(full[:, 128:], fold)))
        mass = jnp.sum(weights, axis=1, keepdims=True)
        masses += [column_to_row(mass[64 * i : 64 * i + 64]) for i in range(4)]
    row = iota((8, 128), 0)
    mesh = mesh_ref[0, 0]
    number = jnp.where(row == 1, ((mesh >> 1) + 1).astype(F32), 0.0)
    tails = [jnp.where(row == 0, mass, jnp.where(row == 2, low_part(mass), number))[None] for mass in masses]
    packed = [jnp.concatenate(tables, axis=0), jnp.concatenate(grads, axis=0), jnp.concatenate(tails, axis=0)]
    packed = jnp.concatenate(packed, axis=1)
    odd = (mesh & 1).astype(F32)
    send_ref[...] = jnp.concatenate([packed * (1.0 - odd), packed * odd], axis=0).astype(BF16)


def dense_kernel(blocks_ref, out_ref):
    blocks = blocks_ref[...].astype(F32)
    numbers = blocks[:, 33:34, :]
    row = iota((40, 128), 0)
    for k in range(OWNERS):
        total = jnp.sum(jnp.where(numbers == float(k + 1), blocks, 0.0), axis=0)
        mass = total[32:33] + total[34:35]
        total = jnp.where(row == 32, mass, jnp.where(row == 34, low_part(mass), total))
        out_ref[k] = total.astype(BF16)


def attend_kernel(sums_ref, qkv_ref, out_ref, token_ref, d_qkv_ref):
    sums = jnp.sum(sums_ref[...].astype(F32), axis=0)
    w_qkv = qkv_ref[...]
    mass = row_to_column(sums[32:33, :] + sums[34:35, :])
    inv = 1.0 / (mass + EPS_MASS)

    def unfold(spread):
        return (spread[:, 0:32] + spread[:, 32:64]) + (spread[:, 64:96] + spread[:, 96:128])

    token = unfold(spread_rows(sums[None, 0:16, :])) * inv
    d_mixed = unfold(spread_rows(sums[None, 16:32, :])).astype(BF16).astype(F32)
    scale = 1.0 / math.sqrt(DH)
    query = dot(token, w_qkv[:, 0:32], precision=HIGHEST)
    keys = dot(token, w_qkv[:, 32:64], precision=HIGHEST)
    values = dot(token, w_qkv[:, 64:96], precision=HIGHEST)
    expo = jnp.exp(dot(query, keys, ((1,), (1,)), HIGHEST) * scale)
    probs = expo / jnp.sum(expo, axis=-1, keepdims=True)
    mixed = dot(probs, values, precision=HIGHEST)
    d_values = dot(probs, d_mixed, ((0,), (0,)), HIGHEST)
    d_probs = dot(d_mixed, values, ((1,), (1,)), HIGHEST)
    d_scores = probs * (d_probs - jnp.sum(probs * d_probs, axis=-1, keepdims=True)) * scale
    d_query = dot(d_scores, keys, precision=HIGHEST)
    d_keys = dot(d_scores, query, ((0,), (0,)), HIGHEST)
    d_qkv = jnp.concatenate([d_query, d_keys, d_values], axis=1)
    token_ref[...] = token
    d_qkv_ref[...] = d_qkv
    d_token = dot(d_qkv, w_qkv, ((1,), (1,)), HIGHEST)
    d_table = d_token * inv
    d_mass = -jnp.sum(d_token * token, axis=1, keepdims=True) * inv

    def pack(values):
        return pack_rows(jnp.concatenate([values] * 4, axis=1))[0]

    tail = column_to_row(d_mass)
    row = iota((8, 128), 0)
    tail = jnp.where(row == 0, tail, jnp.where(row == 2, low_part(tail), 0.0))
    packed = jnp.concatenate([pack(mixed), pack(d_table), tail], axis=0).astype(BF16)
    out_ref[...] = jnp.broadcast_to(packed[None], (OWNERS, 40, 128))


def choose_kernel(blocks_ref, meshes_ref, out_ref):
    numbers = blocks_ref[...].astype(F32)[:, 33:34, :]
    meshes = meshes_ref[...].astype(F32)
    for b in range(2 * HEADS):
        chosen = jnp.zeros((40, 128), F32)
        for k in range(OWNERS):
            chosen = jnp.where(numbers[b] == float(k + 1), meshes[k], chosen)
        out_ref[b] = chosen.astype(BF16)


def back_kernel(
    normed_ref, mid_ref, feat_ref, sw_ref, dout_ref, scaled_ref, weights_ref, g_ref, blocks_ref, temper_ref, tokens_ref,
    mine_ref, other_ref, dmid_ref, dfeat_ref, slice_ref, heat_ref,
):
    tokens = jnp.sum(tokens_ref[...].astype(F32).reshape(2, HEADS, 40, 128), axis=0)
    blocks = blocks_ref[...]
    fold = fold_matrix()
    diagonal = (iota((256, 128), 0) >> 6) == (iota((256, 128), 1) >> 5)
    low_half = iota((1, 128), 1) < 64
    feat = feat_ref[...]
    d_out = dout_ref[...]
    outs, d_mids, d_feats, slabs = [], [], [], []
    temper_grad = jnp.zeros((1, 128), F32)
    lane = iota((1, 128), 1)

    def block_of(packed):
        tiled = dot(spread_rows(packed).astype(BF16), fold)
        return jnp.where(diagonal, tiled, 0.0).astype(BF16)

    for group in range(2):
        lanes = slice(group * 128, (group + 1) * 128)
        wide = slice(group * 256, (group + 1) * 256)
        heads = tokens[4 * group : 4 * group + 4]
        chosen = jnp.concatenate([block_of(heads[:, 0:16]), block_of(heads[:, 16:32])], axis=1)
        d_mass = jnp.concatenate([row_to_column(heads[i, 32:33, :] + heads[i, 34:35, :]) for i in range(4)], axis=0)
        pair = dot(chosen, sw_ref[wide, :], ((0,), (0,)))
        outs.append(pair[:128].astype(BF16))
        d_feats.append(pair[128:].astype(BF16))
        left = jnp.concatenate([d_out[:, lanes], feat[:, lanes]], axis=1)
        d_sw = dot(chosen, left, ((1,), (1,))).astype(BF16).astype(F32)
        d_weights = d_sw + d_mass
        inv_temper = temper_ref[wide, :]
        weights = weights_ref[wide, :]
        d_scaled = weights * (d_weights - head_sums(weights * d_weights))
        products = jnp.sum((d_scaled * scaled_ref[wide, :]).reshape(4, SLICES, ROWS), axis=1)
        totals = jnp.sum(products, axis=1, keepdims=True)
        for i in range(4):
            total = -totals[i : i + 1] * inv_temper[64 * i : 64 * i + 1]
            temper_grad = jnp.where(lane == 4 * group + i, total, temper_grad)
        d_logits = (d_scaled * inv_temper).astype(BF16)
        d_block = dot(mid_ref[lanes, :], d_logits, ((1,), (1,)))
        for i in range(4):
            slabs.append(d_block[i * 32 : (i + 1) * 32, (i // 2) * 128 : (i // 2 + 1) * 128])
        d_mids.append(dot(blocks, d_logits).astype(BF16))
    heat_ref[...] = temper_grad
    slice_ref[...] = jnp.where(
        low_half, (slabs[0] + slabs[2]) + (slabs[4] + slabs[6]), (slabs[1] + slabs[3]) + (slabs[5] + slabs[7])
    )
    d_mid = jnp.concatenate(d_mids, axis=0)
    d_feat = jnp.concatenate(d_feats, axis=0)
    dmid_ref[...] = d_mid
    dfeat_ref[...] = d_feat
    out_grad = dot(jnp.concatenate(outs, axis=0), g_ref[...])
    in_grads = dot(normed_ref[...], jnp.concatenate([d_mid, d_feat], axis=0), ((0,), (1,)))
    halves = []
    for lanes in (slice(0, 128), slice(128, 256)):
        pieces = [out_grad[:, lanes], in_grads[:, :256][:, lanes], in_grads[:, 256:][:, lanes]]
        halves.append(jnp.concatenate([piece.reshape(PEERS, SHARE, 128) for piece in pieces], axis=1))
    first = lax.axis_index("c") == 0
    mine_ref[...] = jnp.where(first, halves[0], halves[1]).astype(BF16)
    other_ref[...] = jnp.where(first, halves[1], halves[0]).astype(BF16)


def norm_kernel(
    dmid_ref, dfeat_ref, wx_ref, wfx_ref, xhat_ref, rstd_ref, gain_ref, g_ref, slice_ref, heat_ref, token_ref, d_qkv_ref,
    feats_ref, small_ref,
):
    d_normed = dot(dmid_ref[...], wx_ref[...], ((0,), (1,))) + dot(dfeat_ref[...], wfx_ref[...], ((0,), (1,)))
    d_normed = d_normed.astype(BF16).astype(F32)
    xhat = xhat_ref[...]
    gain_grad = jnp.sum(d_normed * xhat, axis=0, keepdims=True)
    d_xhat = d_normed * gain_ref[...]
    d_x = rstd_ref[...] * (
        d_xhat
        - jnp.mean(d_xhat, axis=-1, keepdims=True)
        - xhat * jnp.mean(d_xhat * xhat, axis=-1, keepdims=True)
    )
    feats_ref[...] = (g_ref[...].astype(F32) + d_x).astype(BF16)
    qkv_grad = dot(token_ref[...], d_qkv_ref[...], ((0,), (0,)), HIGHEST)
    row = iota((8, 128), 0)
    vectors = jnp.where(row == 0, gain_grad[:, :128], jnp.where(row == 1, gain_grad[:, 128:], 0.0))
    small_ref[0:32, :] = slice_ref[...]
    small_ref[32:64, :] = jnp.concatenate([qkv_grad, jnp.zeros((DH, 32), F32)], axis=1)
    small_ref[64:72, :] = jnp.where(row == 2, heat_ref[...], vectors)
    small_ref[72:, :] = jnp.zeros((WIDTH - 72, 128), F32)


def add_kernel(a_ref, b_ref, small_ref, out_ref):
    total = a_ref[...].astype(F32) + b_ref[...].astype(F32)
    small = small_ref[...].reshape(PEERS, SHARE, 128)
    out_ref[...] = jnp.concatenate([total, small], axis=1).astype(BF16)


def sum_kernel(parts_ref, out_ref):
    total = jnp.sum(parts_ref[...].astype(F32), axis=0).astype(BF16)
    out_ref[...] = jnp.broadcast_to(total[None], out_ref.shape)


def finish_kernel(
    parts_ref,
    gain_hbm, in_x_hbm, in_fx_hbm, slice_hbm, temper_hbm, qkv_hbm, out_hbm,
    gain_ref, in_x_ref, in_fx_ref, slice_ref, temper_ref, qkv_ref, out_ref, sems,
):
    copies = []

    def leave(source, target):
        copies.append(pltpu.make_async_copy(source, target, sems.at[len(copies)]))

    for at, (ref, hbm) in enumerate(((out_ref, out_hbm), (in_x_ref, in_x_hbm), (in_fx_ref, in_fx_hbm))):
        for half in range(2):
            piece = parts_ref[half * PEERS : (half + 1) * PEERS].astype(F32)[:, at * SHARE : (at + 1) * SHARE]
            ref[:, half * 128 : (half + 1) * 128] = piece.reshape(WIDTH, 128)
        leave(ref, hbm)
    small = parts_ref[:PEERS].astype(F32)[:, 3 * SHARE :] + parts_ref[PEERS:].astype(F32)[:, 3 * SHARE :]
    small = small.reshape(WIDTH, 128)
    slices = small[0:32]
    slice_ref[...] = slices[:, :64] + slices[:, 64:]
    leave(slice_ref, slice_hbm)
    qkv_ref[...] = small[32:64, :96]
    leave(qkv_ref, qkv_hbm)
    gain_ref[:, :128] = small[64:65]
    gain_ref[:, 128:] = small[65:66]
    leave(gain_ref, gain_hbm)
    temper_ref[...] = small[66:67, :8]
    leave(temper_ref, temper_hbm)
    for copy in copies:
        copy.start()
    for copy in copies:
        copy.wait()


def call(kernel, name, inputs, outputs, scalars=0, far_in=False, far_out=False, scratch=(), cost=None):
    single = not isinstance(outputs, (list, tuple))
    in_spec = pl.BlockSpec(memory_space=pltpu.HBM if far_in else pltpu.VMEM)
    out_spec = pl.BlockSpec(memory_space=pltpu.HBM if far_out else pltpu.VMEM)
    return pl.pallas_call(
        kernel,
        name=name,
        out_shape=outputs,
        in_specs=[pl.BlockSpec(memory_space=pltpu.SMEM)] * scalars + [in_spec] * (len(inputs) - scalars),
        out_specs=out_spec if single else [out_spec] * len(outputs),
        scratch_shapes=scratch,
        compiler_params=pltpu.CompilerParams(vmem_limit_bytes=48 * 1024 * 1024),
        cost_estimate=cost,
    )(*inputs)


def shape(dims, dtype=BF16):
    return jax.ShapeDtypeStruct(dims, dtype)


def shards(
    node_feats, cotangent, mesh_of_block, block_rows, ln_gain, w_in_x, w_in_fx, w_slice, temper, w_qkv, w_out
):
    x = node_feats.reshape(ROWS, WIDTH)
    cot = cotangent.reshape(ROWS, WIDTH)
    gain = ln_gain.reshape(1, WIDTH)
    wide = shape((ROWS, WIDTH))
    packets = shape((2 * HEADS, 40, 128))
    owned = shape((OWNERS, 40, 128))
    tall = shape((2 * WIDTH, ROWS), F32)
    flat = shape((WIDTH, ROWS))
    inputs = (x, gain, w_in_x, w_in_fx, w_slice, temper.reshape(1, HEADS), cot, w_out)
    far = [pltpu.with_memory_space_constraint(a, pltpu.HBM) for a in inputs]
    scratch = [pltpu.VMEM(a.shape, a.dtype) for a in (x, w_slice, inputs[5], cot, w_out)]
    scratch.append(pltpu.SemaphoreType.DMA((len(far),)))
    send, normed, mid, feat, sw, d_out, scaled, weights, xhat, rstd, gains, wx, wfx, g, diagonal, heat = call(
        front_kernel,
        "front",
        (block_rows, mesh_of_block, *far),
        [
            packets, wide, flat, wide, shape((2 * WIDTH, ROWS)), wide,
            tall, tall, shape((ROWS, WIDTH), F32), shape((ROWS, 1), F32),
            shape((1, WIDTH), F32), shape((WIDTH, WIDTH)), shape((WIDTH, WIDTH)), wide,
            shape((128, 256)), shape((2 * WIDTH, 1), F32),
        ],
        scalars=2,
        far_in=True,
        scratch=scratch,
    )
    blocks = lax.all_to_all(send, ("zl", "y", "c"), 0, 0)
    dense = call(dense_kernel, "dense", (blocks,), owned)
    sums = lax.all_to_all(dense, ("zb", "zc", "za"), 0, 0)
    answer, token, d_qkv = call(
        attend_kernel,
        "attend",
        (sums, w_qkv),
        [owned, shape((SLICES, DH), F32), shape((SLICES, 3 * DH), F32)],
    )
    meshes = lax.all_to_all(answer, ("zb", "zc", "za"), 0, 0)
    chosen = call(choose_kernel, "choose", (blocks, meshes), packets)
    tokens = lax.all_to_all(chosen, ("zl", "y", "c"), 0, 0)
    share = shape((PEERS, 4 * SHARE, 128))
    big = shape((PEERS, 3 * SHARE, 128))
    mine, other, d_mid, d_feat, slice_grad, temper_grad = call(
        back_kernel,
        "back",
        (normed, mid, feat, sw, d_out, scaled, weights, g, diagonal, heat, tokens),
        [big, big, flat, flat, shape((DH, 128), F32), shape((1, 128), F32)],
    )
    other = lax.ppermute(other, "c", [(0, 1), (1, 0)])
    feats_grad, small = call(
        norm_kernel,
        "norm",
        (d_mid, d_feat, wx, wfx, xhat, rstd, gains, g, slice_grad, temper_grad, token, d_qkv),
        [wide, shape((WIDTH, 128), F32)],
        cost=pl.CostEstimate(flops=4 * ROWS * WIDTH * WIDTH, bytes_accessed=4 * 1024 * 1024, transcendentals=0),
    )
    across = ("y", "zl", "x")
    parts = call(add_kernel, "add_pair", (mine, other, small), share)
    parts = lax.all_to_all(parts, across, 0, 0)
    parts = call(sum_kernel, "sum_peers", (parts,), shape((OWNERS, 4 * SHARE, 128)))
    parts = lax.all_to_all(parts, ("zb", "zc", "za"), 0, 0)
    parts = call(sum_kernel, "sum_z", (parts,), share)
    parts = lax.all_to_all(parts, across, 0, 0)
    parts = lax.all_gather(parts, "c", axis=0, tiled=True)
    square = shape((WIDTH, WIDTH), F32)
    results = [
        shape((1, WIDTH), F32), square, square, shape((DH, SLICES), F32),
        shape((1, HEADS), F32), shape((DH, 3 * DH), F32), square,
    ]
    gain_grad, in_x_grad, in_fx_grad, slice_grad, temper_grad, qkv_grad, out_grad = call(
        finish_kernel,
        "finish",
        (parts,),
        results,
        far_out=True,
        scratch=[pltpu.VMEM(r.shape, r.dtype) for r in results] + [pltpu.SemaphoreType.DMA((len(results),))],
    )
    return (
        feats_grad.reshape(1, 1, ROWS, WIDTH),
        gain_grad.reshape(WIDTH),
        in_x_grad,
        in_fx_grad,
        slice_grad,
        temper_grad.reshape(HEADS),
        qkv_grad,
        out_grad,
    )


def solution(mesh):
    groups = mesh.shape["dp"]
    devices = mesh.devices.reshape(4, 2, 2, 2, 2, 2, groups)
    grid = Mesh(devices, ("y", "za", "zb", "zc", "zl", "c", "x"))
    node = ("y", "za", "zb", "zc", "zl", "c")
    blocks = P("x", node, None, None)
    scalars = P("x", node)
    return jax.shard_map(
        shards,
        mesh=grid,
        in_specs=(blocks, blocks, scalars, scalars) + (P(),) * 7,
        out_specs=(blocks,) + (P(),) * 7,
        check_vma=False,
    )
```
